128 devices in a mesh: section: 4 (over x), dp: 16 (over z, y), tensor: 2 (over core).
Axes of the slice: x: 4, y: 4, z: 4, core: 2. Of those that a mesh axis runs over, the one named last changes fastest.
Arguments:
- carried: bfloat16 [4, 4096, 8192], P('section', 'dp', 'tensor'), may hold values from -448 to 448
- norm_gain: float32 [4, 8192], P('section'), may hold values from 0.5 to 1.5
- frozen_key_matrix: bfloat16 [4, 8192, 1024], P('section', None, 'tensor'), may hold values from -0.044194174 to 0.044194174
- frozen_value_matrix: bfloat16 [4, 8192, 1024], P('section', None, 'tensor'), may hold values from -0.044194174 to 0.044194174
- adapter_params: float32 [4, 2, 8192, 256], P('section', None, ('dp', 'tensor')), may hold values from -0.08 to 0.08
- adapter_second: float32 [4, 8192, 256], P('section', ('dp', 'tensor')), may hold values from 0.003 to 0.03
- right_params: float32 [4, 2, 128, 2, 1024], P('section', None, 'dp', None, 'tensor'), may hold values from -0.2 to 0.2
- right_second: float32 [4, 128, 2, 1024], P('section', 'dp', None, 'tensor'), may hold values from 0.003 to 0.03
- row_jobs: int32 [4, 4096], P('section', 'dp'), may hold values from 0 to 7
- job_tokens: int32 [8], replicated, may hold values from 512 to 1023
- finishing: int32 [4], P('section'), may hold values from 0 to 7
- cotangent: bfloat16 [4, 4096, 2, 1024], P('section', 'dp', None, 'tensor'), may hold values from -6 to 6
Outputs:
- kv_out: bfloat16 [4, 4096, 2, 1024], P('section', 'dp', None, 'tensor')
- input_grad: bfloat16 [4, 4096, 8192], P('section', 'dp', 'tensor')
- new_adapter: float32 [4, 3, 8192, 256], P('section', None, ('dp', 'tensor'))
- new_right: float32 [4, 3, 128, 2, 1024], P('section', None, 'dp', None, 'tensor')
- checkpoint: float32 [4, 3, 32, 8192], P('section', None, None, 'dp')
The draws below stay inside these ranges and needn't reach their ends.
All inputs are finite; a program needn't handle non-finite values.
Results may differ from the reference program's by a relative error of at most 0.011.
Values may be sent and summed in bfloat16 or wider, within the bound.
No kernel may reach another device: no remote copies, remote signals or barrier semaphores. Data moves between devices by JAX's collectives and lax.ppermute only.
A program may use at most 192 MiB of HBM per device.

```python
import math
import jax
import jax.numpy as jnp
import numpy as np
from jax import lax

D = 8192
JOBS = 8
RANK = 16
ADAM_STEP = 10
KV = 1024
TOKENS = 4096
N_SECTION = 4


def shared_input(key, row_top):
    random_part = jnp.clip(jax.random.normal(jax.random.fold_in(key, 101), (N_SECTION, TOKENS, D), jnp.float32), -4.0, 4.0)
    position = (jnp.arange(D, dtype=jnp.float32) + 0.5) / D
    ramp_level = 0.5 + (position - 0.5)
    jitter = jax.random.uniform(jax.random.fold_in(key, 102), (N_SECTION, 1, D), jnp.float32, 0.7, 1.4)
    feature_scale = jnp.exp(math.log(10.0) * ramp_level)[None, None, :] * jitter
    row_level = jax.random.uniform(jax.random.fold_in(key, 103), (N_SECTION, TOKENS, 1), jnp.float32, 0.0, 1.0)
    row_scale = jnp.exp(row_level * math.log(row_top))
    return random_part * feature_scale * row_scale


def shared_frozen(key, matrix_index):
    values = jnp.clip(jax.random.normal(jax.random.fold_in(key, 201 + matrix_index), (N_SECTION, D, KV), jnp.float32), -4.0, 4.0)
    return values * D ** (-0.5)


def draw_carried(key, part):
    row_top = 4.0
    inputs = shared_input(key, row_top)
    return inputs.astype(jnp.bfloat16)


def draw_frozen_key_matrix(key, part):
    values = shared_frozen(key, 0)
    return values.astype(jnp.bfloat16)


def draw_frozen_value_matrix(key, part):
    values = shared_frozen(key, 1)
    return values.astype(jnp.bfloat16)


def draw_cotangent(key, part):
    row_top = 4.0
    inputs = shared_input(key, row_top)
    key_matrix = shared_frozen(key, 0)
    value_matrix = shared_frozen(key, 1)
    key = jax.random.fold_in(key, 4)
    previous = jnp.roll(inputs, 1, axis=0)
    normalized = previous * lax.rsqrt(jnp.mean(previous * previous, axis=2, keepdims=True) + 1e-05)
    key_target = jnp.einsum('std,sdk->stk', normalized, key_matrix, precision=lax.Precision.HIGHEST)
    value_target = jnp.einsum('std,sdk->stk', normalized, value_matrix, precision=lax.Precision.HIGHEST)
    targets = jnp.stack([key_target, value_target], axis=2)
    random_part = jax.random.normal(key, targets.shape, jnp.float32)
    return jnp.clip(targets + random_part, -6.0, 6.0).astype(jnp.bfloat16)


def draw_adapter_params(key, part):
    key = jax.random.fold_in(key, 11)
    factor_key, moment_key = jax.random.split(key)
    shape = (N_SECTION, D, 2 * JOBS * RANK)
    factors = jnp.clip(jax.random.normal(factor_key, shape, jnp.float32), -4.0, 4.0) * 0.02
    moments = jnp.clip(jax.random.normal(moment_key, shape, jnp.float32), -4.0, 4.0) * 0.002
    return jnp.stack([factors, moments], axis=1)


def draw_right_params(key, part):
    key = jax.random.fold_in(key, 12)
    factor_key, moment_key = jax.random.split(key)
    shape = (N_SECTION, JOBS * RANK, 2, KV)
    factors = jnp.clip(jax.random.normal(factor_key, shape, jnp.float32), -4.0, 4.0) * 0.05
    moments = jnp.clip(jax.random.normal(moment_key, shape, jnp.float32), -4.0, 4.0) * 0.003
    return jnp.stack([factors, moments], axis=1)


def set_ends(drawn, stream_key, smallest, largest):
    shape = drawn.shape
    place = [jax.random.randint(jax.random.fold_in(stream_key, axis), (), 0, shape[axis]) for axis in range(len(shape))]
    drawn = drawn.at[tuple(place)].set(smallest)
    longest = shape.index(max(shape))
    place[longest] = (place[longest] + 1) % shape[longest]
    return drawn.at[tuple(place)].set(largest)


def block_scale(key, dims, shards, smallest, top_value):
    gain, own = 1.0, jax.random.fold_in(key, 6)
    for axis_at, parts in shards:
        draws = jnp.exp(jax.random.uniform(jax.random.fold_in(own, axis_at), (parts,), jnp.float32, smallest / len(shards), top_value / len(shards)))
        gain = gain * jnp.repeat(draws, dims[axis_at] // parts).reshape([-1 if axis == axis_at else 1 for axis in range(len(dims))])
    return gain


def rank_table(count, slope):
    loads = [(1 << 20) // math.isqrt(rank ** slope) + 1 for rank in range(1, count + 1)]
    deviation = 1 + sum(loads) // (1 << 30)
    return np.cumsum(np.array([max(1, weight // deviation) for weight in loads]))


def skewed_ids(rng, shape, number_of, lean):
    grid = rank_table(number_of, lean)
    ticket = jax.random.randint(jax.random.fold_in(rng, 1), shape, 0, int(grid[number_of - 1]))
    standing = jnp.searchsorted(jnp.asarray(grid, jnp.int32), ticket, side="right")
    return jax.random.permutation(jax.random.fold_in(rng, 2), number_of)[standing].astype(jnp.int32)


def setup_inputs(seed: int = 0) -> dict:
    key_of = jax.random.split(jax.random.key(seed), 13)
    carried = draw_carried(jax.random.fold_in(key_of[12], 71), 0)
    norm_gain = jnp.clip(1.0 + 0.1 * jax.random.normal(key_of[1], (N_SECTION, D), jnp.float32), 0.5, 1.5)
    frozen_key_matrix = draw_frozen_key_matrix(jax.random.fold_in(key_of[12], 71), 0)
    frozen_value_matrix = draw_frozen_value_matrix(jax.random.fold_in(key_of[12], 71), 0)
    adapter_params = draw_adapter_params(jax.random.fold_in(key_of[12], 71), 0)
    adapter_second = jnp.clip(jnp.exp(math.log(0.03) - 2.3025851 * jax.random.uniform(key_of[5], (N_SECTION, D, 2 * JOBS * RANK), jnp.float32) ** block_scale(key_of[5], (N_SECTION, D, 2 * JOBS * RANK), ((0, 4), (1, 32)), -0.2, 0.2)), 0.003, 0.03)
    right_params = draw_right_params(jax.random.fold_in(key_of[12], 71), 0)
    right_second = jnp.clip(jnp.exp(math.log(0.03) - 2.3025851 * jax.random.uniform(key_of[7], (N_SECTION, JOBS * RANK, 2, KV), jnp.float32) ** block_scale(key_of[7], (N_SECTION, JOBS * RANK, 2, KV), ((0, 4), (1, 16), (3, 2)), -0.2, 0.2)), 0.003, 0.03)
    row_jobs = set_ends(skewed_ids(key_of[8], (N_SECTION, TOKENS), JOBS, 2), jax.random.fold_in(key_of[8], 3), 0, JOBS - 1).astype(jnp.int32)
    job_tokens = set_ends(jax.random.randint(key_of[9], (JOBS,), TOKENS // JOBS, 2 * TOKENS // JOBS), jax.random.fold_in(key_of[9], 1), TOKENS // JOBS, (2 * TOKENS // JOBS) - 1).astype(jnp.int32)
    finishing = set_ends(jax.random.randint(key_of[10], (N_SECTION,), 0, JOBS), jax.random.fold_in(key_of[10], 1), 0, JOBS - 1).astype(jnp.int32)
    cotangent = draw_cotangent(jax.random.fold_in(key_of[12], 71), 0)
    return {"carried": carried, "norm_gain": norm_gain, "frozen_key_matrix": frozen_key_matrix, "frozen_value_matrix": frozen_value_matrix, "adapter_params": adapter_params, "adapter_second": adapter_second, "right_params": right_params, "right_second": right_second, "row_jobs": row_jobs, "job_tokens": job_tokens, "finishing": finishing, "cotangent": cotangent}


ADAPTER_SCALING = 2.0
BETA_ONE = 0.9
BETA_TWO = 0.999
ADAM_EPS = 1e-08
LEARN_RATE = 0.01

def adam_update(param, first, second, grad):
    first = BETA_ONE * first + (1.0 - BETA_ONE) * grad
    second = BETA_TWO * second + (1.0 - BETA_TWO) * grad * grad
    first_fix = 1.0 - BETA_ONE ** ADAM_STEP
    second_fix = 1.0 - BETA_TWO ** ADAM_STEP
    param = param - LEARN_RATE * (first / first_fix) / (jnp.sqrt(second / second_fix) + ADAM_EPS)
    return jnp.stack([param, first, second])

def contracted_rows(left, right):
    return lax.dot_general(left, right, (((0,), (0,)), ((), ())), preferred_element_type=jnp.float32)

def contracted_columns(left, right):
    return lax.dot_general(left, right, (((1,), (1,)), ((), ())), preferred_element_type=jnp.float32)

def reference(carried, norm_gain, frozen_key_matrix, frozen_value_matrix, adapter_params, adapter_second, right_params, right_second, row_jobs, job_tokens, finishing, cotangent):
    feature_width = JOBS * RANK
    columns = 2 * feature_width
    col_job = jnp.arange(columns, dtype=jnp.int32) % feature_width // RANK
    job_ids = jnp.arange(JOBS, dtype=jnp.int32)
    counts = job_tokens.astype(jnp.float32)
    column_total = lax.optimization_barrier(jnp.sum(jnp.where(col_job[:, None] == job_ids[None, :], counts[None, :], 0.0), axis=1))
    row_job = jnp.arange(feature_width, dtype=jnp.int32) // RANK
    row_count = lax.optimization_barrier(jnp.sum(jnp.where(row_job[:, None] == job_ids[None, :], counts[None, :], 0.0), axis=1))
    kv_list, gradient_collection, adapter_list, right_list, check_list = ([], [], [], [], [])
    for current_portion in range(N_SECTION):
        complete_input = carried[(current_portion - 1) % N_SECTION].astype(jnp.float32)
        inverse_deviation = lax.rsqrt(lax.optimization_barrier(jnp.mean(complete_input * complete_input, axis=1, keepdims=True)) + 1e-05)
        centered_normalized_input = complete_input * inverse_deviation
        norm_gain_weight = norm_gain[current_portion]
        normalized_input = (centered_normalized_input * norm_gain_weight[None, :]).astype(jnp.bfloat16)
        adapter_factors = adapter_params[current_portion, 0].astype(jnp.bfloat16)
        upper_bound_index = right_params[current_portion, 0].astype(jnp.bfloat16)
        mask = row_jobs[current_portion][:, None] == col_job[None, :]
        lower_bound_index = jnp.where(mask, jnp.dot(normalized_input, adapter_factors, preferred_element_type=jnp.float32), 0.0).astype(jnp.bfloat16)
        key_rows = jnp.dot(normalized_input, frozen_key_matrix[current_portion], preferred_element_type=jnp.float32) + ADAPTER_SCALING * jnp.dot(lower_bound_index[:, :feature_width], upper_bound_index[:, 0], preferred_element_type=jnp.float32)
        value_rows = jnp.dot(normalized_input, frozen_value_matrix[current_portion], preferred_element_type=jnp.float32) + ADAPTER_SCALING * jnp.dot(lower_bound_index[:, feature_width:], upper_bound_index[:, 1], preferred_element_type=jnp.float32)
        kv_list.append(jnp.stack([key_rows, value_rows], axis=1).astype(jnp.bfloat16))
        key_gradient = cotangent[current_portion, :, 0]
        value_gradient = cotangent[current_portion, :, 1]
        backward_output = jnp.concatenate([contracted_columns(key_gradient, upper_bound_index[:, 0]), contracted_columns(value_gradient, upper_bound_index[:, 1])], axis=1)
        backward_output = jnp.where(mask, backward_output, 0.0).astype(jnp.bfloat16)
        down_weight_gradient = ADAPTER_SCALING * contracted_rows(normalized_input, backward_output) / column_total[None, :]
        up_weight_gradient = ADAPTER_SCALING * jnp.stack([contracted_rows(lower_bound_index[:, :feature_width], key_gradient), contracted_rows(lower_bound_index[:, feature_width:], value_gradient)], axis=1)
        up_weight_gradient = up_weight_gradient / row_count[:, None, None]
        normed_input_gradient = contracted_columns(key_gradient, frozen_key_matrix[current_portion]) + contracted_columns(value_gradient, frozen_value_matrix[current_portion]) + ADAPTER_SCALING * contracted_columns(backward_output, adapter_factors)
        scaled_output = norm_gain_weight[None, :] * normed_input_gradient
        norm_statistic = lax.optimization_barrier(jnp.mean(scaled_output * centered_normalized_input, axis=1, keepdims=True))
        gradient_collection.append((inverse_deviation * (scaled_output - centered_normalized_input * norm_statistic)).astype(jnp.bfloat16))
        new_a = adam_update(adapter_params[current_portion, 0], adapter_params[current_portion, 1], adapter_second[current_portion], down_weight_gradient)
        new_b = adam_update(right_params[current_portion, 0], right_params[current_portion, 1], right_second[current_portion], up_weight_gradient)
        adapter_list.append(new_a)
        right_list.append(new_b)
        split = new_a.reshape(3, D, 2, JOBS, RANK)
        picked = lax.dynamic_index_in_dim(split, finishing[current_portion], axis=3, keepdims=False)
        check_list.append(jnp.transpose(picked, (0, 2, 3, 1)).reshape(3, 2 * RANK, D))
    input_grad = jnp.stack([gradient_collection[(current_portion + 1) % N_SECTION] for current_portion in range(N_SECTION)])
    return (jnp.stack(kv_list), input_grad, jnp.stack(adapter_list), jnp.stack(right_list), jnp.stack(check_list))
```

```python
import jax
import jax.numpy as jnp
from jax import lax
from jax.sharding import PartitionSpec as P

JOBS = 8
RANK = 16
ADAM_STEP = 10
ADAPTER_SCALING = 2.0
BETA_ONE = 0.9
BETA_TWO = 0.999
ADAM_EPS = 1e-08
LEARN_RATE = 0.01

SIDE = 4
CHUNKS = 2


def shifted(value, axis, steps):
    count = lax.axis_size(axis)
    pairs = [(source, (source + steps) % count) for source in range(count)]
    return lax.ppermute(value, axis, pairs)


def swapped(value):
    return shifted(value, "tensor", 1)


def shifted_y(value, steps):
    pairs = [
        (z * SIDE + y, z * SIDE + (y + steps) % SIDE) for z in range(SIDE) for y in range(SIDE)
    ]
    return lax.ppermute(value, "dp", pairs)


def shifted_z(value, steps):
    pairs = [
        (z * SIDE + y, (z + steps) % SIDE * SIDE + y) for z in range(SIDE) for y in range(SIDE)
    ]
    return lax.ppermute(value, "dp", pairs)


def gathered_ring(value, shift, position):
    later = [shift(value, 3), shift(value, 2), shift(value, 1), value]
    twice = jnp.stack(later + later)
    return lax.dynamic_slice_in_dim(twice, SIDE - 1 - position, SIDE, 0)


def adam_update(param, first, second, grad):
    first = BETA_ONE * first + (1.0 - BETA_ONE) * grad
    second = BETA_TWO * second + (1.0 - BETA_TWO) * grad * grad
    first_fix = 1.0 - BETA_ONE**ADAM_STEP
    second_fix = 1.0 - BETA_TWO**ADAM_STEP
    param = param - LEARN_RATE * (first / first_fix) / (jnp.sqrt(second / second_fix) + ADAM_EPS)
    return jnp.stack([param, first, second])


def rows_dot(left, right):
    return lax.dot_general(
        left, right, (((0,), (0,)), ((), ())), preferred_element_type=jnp.float32
    )


def columns_dot(left, right):
    return lax.dot_general(
        left, right, (((1,), (1,)), ((), ())), preferred_element_type=jnp.float32
    )


def dot(left, right):
    return jnp.dot(left, right, preferred_element_type=jnp.float32)


def local(
    carried,
    norm_gain,
    frozen_key_matrix,
    frozen_value_matrix,
    adapter_params,
    adapter_second,
    right_params,
    right_second,
    row_jobs,
    job_tokens,
    finishing,
    cotangent,
):
    n_data = lax.axis_size("dp")
    core = lax.axis_index("tensor")
    place = lax.axis_index("dp")
    feature_width = JOBS * RANK
    columns = 2 * feature_width
    x_here = carried[0]
    tokens, half = x_here.shape
    width = 2 * half
    block = adapter_params.shape[2]
    gain = norm_gain[0]
    key_matrix, value_matrix = frozen_key_matrix[0], frozen_value_matrix[0]
    key_gradient, value_gradient = cotangent[0, :, 0], cotangent[0, :, 1]
    own = core == 0

    def by_core(value, axis):
        other = swapped(value)
        first = jnp.where(own, value, other)
        second = jnp.where(own, other, value)
        return jnp.concatenate([first, second], axis=axis)

    x_in = shifted(x_here, "section", 1)
    factors = adapter_params[0, 0].astype(jnp.bfloat16)
    factors_next = shifted(factors, "section", -1)
    gain_next = shifted(gain, "section", -1)
    both = lax.all_gather(
        jnp.concatenate([factors, factors_next], axis=1), "dp", axis=0, tiled=True
    )
    factors_par, factors_next_par = both[:, :columns], both[:, columns:]

    up = right_params[0, 0].astype(jnp.bfloat16)
    up = gathered_ring(up, shifted_y, place % SIDE)
    up = gathered_ring(up, shifted_z, place // SIDE)
    up = up.reshape(feature_width, 2, up.shape[-1])
    up_key, up_value = up[:, 0], up[:, 1]

    part = half // CHUNKS
    incoming = []
    for chunk in range(CHUNKS):
        pieces = []
        for side in range(2):
            start = side * half + chunk * part
            piece = columns_dot(
                key_gradient, key_matrix[start : start + part]
            ) + columns_dot(value_gradient, value_matrix[start : start + part])
            pieces.append(piece.astype(jnp.bfloat16))
        leaving = jnp.where(own, pieces[1], pieces[0])
        staying = jnp.where(own, pieces[0], pieces[1])
        gain_part = lax.dynamic_slice_in_dim(gain, core * half + chunk * part, part, 0)
        total = staying.astype(jnp.float32) + swapped(leaving).astype(jnp.float32)
        scaled = (total * gain_part[None, :]).astype(jnp.bfloat16)
        incoming.append(shifted(scaled, "section", -1))

    col_job = jnp.arange(columns, dtype=jnp.int32) % feature_width // RANK
    mask = row_jobs[0][:, None] == col_job[None, :]
    back_part = jnp.concatenate(
        [columns_dot(key_gradient, up_key), columns_dot(value_gradient, up_value)], axis=1
    )
    back = jnp.where(mask, back_part + swapped(back_part), 0.0).astype(jnp.bfloat16)
    back_next = shifted(back, "section", -1)

    x_wide = x_here.astype(jnp.float32)
    squares = jnp.sum(x_wide * x_wide, axis=1, keepdims=True)
    rstd = lax.rsqrt((squares + swapped(squares)) / width + 1e-05)
    rstd_in = shifted(rstd, "section", 1)
    gain_next_half = lax.dynamic_slice_in_dim(gain_next, core * half, half, 0)
    xn_here = (x_wide * rstd * gain_next_half[None, :]).astype(jnp.bfloat16)
    split = xn_here.reshape(tokens, half // (2 * block), 2, block)
    kept = jnp.where(own, split[:, :, 0], split[:, :, 1]).reshape(tokens, half // 2)
    given = jnp.where(own, split[:, :, 1], split[:, :, 0]).reshape(tokens, half // 2)
    taken = swapped(given)
    xn_par = jnp.concatenate(
        [jnp.where(own, kept, taken), jnp.where(own, taken, kept)], axis=1
    )
    down_piece = (ADAPTER_SCALING * rows_dot(xn_par, back_next)).astype(jnp.bfloat16)
    down_pieces = lax.all_to_all(
        down_piece.reshape(n_data, block, columns), "dp", 0, 0, tiled=True
    )
    down_sum = jnp.sum(down_pieces.astype(jnp.float32), axis=0).astype(jnp.bfloat16)
    down_sum = shifted(down_sum, "section", 1).astype(jnp.float32)

    gain_half = lax.dynamic_slice_in_dim(gain, core * half, half, 0)
    xn_half = (x_in.astype(jnp.float32) * rstd_in * gain_half[None, :]).astype(jnp.bfloat16)
    xn = by_core(xn_half, 1)
    xn_blocks = xn.reshape(tokens, n_data, 2, block)
    xn_mine = lax.dynamic_index_in_dim(xn_blocks, core, axis=2, keepdims=False)
    low_part = dot(xn_mine.reshape(tokens, half), factors_par)
    low = jnp.where(mask, low_part + swapped(low_part), 0.0).astype(jnp.bfloat16)
    low_key, low_value = low[:, :feature_width], low[:, feature_width:]
    keys = dot(xn, key_matrix) + ADAPTER_SCALING * dot(low_key, up_key)
    values = dot(xn, value_matrix) + ADAPTER_SCALING * dot(low_value, up_value)
    kv_out = jnp.stack([keys, values], axis=1).astype(jnp.bfloat16)[None]

    up_piece = ADAPTER_SCALING * jnp.stack(
        [rows_dot(low_key, key_gradient), rows_dot(low_value, value_gradient)], axis=1
    )
    up_pieces = up_piece.astype(jnp.bfloat16).reshape(n_data, -1, 2, up.shape[-1])
    up_pieces = lax.all_to_all(up_pieces, "dp", 0, 0, tiled=True)
    up_sum = jnp.sum(up_pieces.astype(jnp.float32), axis=0)

    next_blocks = factors_next_par.reshape(2, half // block // 2, block, columns)
    next_kept = jnp.where(own, next_blocks[0], next_blocks[1])
    next_taken = swapped(jnp.where(own, next_blocks[1], next_blocks[0]))
    factors_half = jnp.stack(
        [jnp.where(own, next_kept, next_taken), jnp.where(own, next_taken, next_kept)], axis=1
    ).reshape(half, columns)
    low_rank = ADAPTER_SCALING * columns_dot(back_next, factors_half)
    scaled = jnp.concatenate(incoming, axis=1).astype(jnp.float32)
    scaled = scaled + gain_next_half[None, :] * low_rank
    xhat = x_wide * rstd
    statistic = jnp.sum(scaled * xhat, axis=1, keepdims=True)
    statistic = (statistic + swapped(statistic)) / width
    input_grad = (rstd * (scaled - xhat * statistic)).astype(jnp.bfloat16)[None]

    job_ids = jnp.arange(JOBS, dtype=jnp.int32)
    counts = job_tokens.astype(jnp.float32)
    column_total = jnp.sum(
        jnp.where(col_job[:, None] == job_ids[None, :], counts[None, :], 0.0), axis=1
    )
    rows_local = up_sum.shape[0]
    row_job = (place * rows_local + jnp.arange(rows_local, dtype=jnp.int32)) // RANK
    row_count = jnp.sum(
        jnp.where(row_job[:, None] == job_ids[None, :], counts[None, :], 0.0), axis=1
    )
    new_a = adam_update(
        adapter_params[0, 0],
        adapter_params[0, 1],
        adapter_second[0],
        down_sum / column_total[None, :],
    )
    new_b = adam_update(
        right_params[0, 0], right_params[0, 1], right_second[0], up_sum / row_count[:, None, None]
    )
    chosen = lax.dynamic_index_in_dim(
        new_a.reshape(3, block, 2, JOBS, RANK), finishing[0], axis=3, keepdims=False
    )
    chosen = jnp.transpose(chosen, (0, 2, 3, 1)).reshape(3, 2 * RANK, block)
    checkpoint = by_core(chosen, 2)[None]
    return (kv_out, input_grad, new_a[None], new_b[None], checkpoint)


def solution(mesh):
    return jax.shard_map(
        local,
        mesh=mesh,
        in_specs=(
            P("section", "dp", "tensor"),
            P("section", None),
            P("section", None, "tensor"),
            P("section", None, "tensor"),
            P("section", None, ("dp", "tensor"), None),
            P("section", ("dp", "tensor"), None),
            P("section", None, "dp", None, "tensor"),
            P("section", "dp", None, "tensor"),
            P("section", "dp"),
            P(),
            P("section"),
            P("section", "dp", None, "tensor"),
        ),
        out_specs=(
            P("section", "dp", None, "tensor"),
            P("section", "dp", "tensor"),
            P("section", None, ("dp", "tensor"), None),
            P("section", None, "dp", None, "tensor"),
            P("section", None, None, "dp"),
        ),
        check_vma=False,
    )
```

```python
import jax
import jax.numpy as jnp
from jax import lax
from jax.experimental import pallas as pl
from jax.experimental.pallas import tpu as pltpu
from jax.sharding import PartitionSpec as P

JOBS = 8
RANK = 16
ADAM_STEP = 10
ADAPTER_SCALING = 2.0
BETA_ONE = 0.9
BETA_TWO = 0.999
ADAM_EPS = 1e-08
LEARN_RATE = 0.01

FEATURE_WIDTH = JOBS * RANK
COLUMNS = 2 * FEATURE_WIDTH
STEP = 1024
SIDE = 4
VMEM_LIMIT = 54 * 1024 * 1024
HINT = 16

F32 = jnp.float32
BF16 = jnp.bfloat16


def shifted(value, axis, steps):
    count = lax.axis_size(axis)
    pairs = [(source, (source + steps) % count) for source in range(count)]
    return lax.ppermute(value, axis, pairs)


def swapped(value):
    return shifted(value, "tensor", 1)


def after(value, *others):
    return lax.optimization_barrier((value,) + others)[0]


def shifted_y(value, steps):
    pairs = [
        (z * SIDE + y, z * SIDE + (y + steps) % SIDE) for z in range(SIDE) for y in range(SIDE)
    ]
    return lax.ppermute(value, "dp", pairs)


def shifted_z(value, steps):
    pairs = [
        (z * SIDE + y, (z + steps) % SIDE * SIDE + y) for z in range(SIDE) for y in range(SIDE)
    ]
    return lax.ppermute(value, "dp", pairs)


def adam_update(param, first, second, grad):
    first = BETA_ONE * first + (1.0 - BETA_ONE) * grad
    second = BETA_TWO * second + (1.0 - BETA_TWO) * grad * grad
    first_fix = 1.0 - BETA_ONE**ADAM_STEP
    second_fix = 1.0 - BETA_TWO**ADAM_STEP
    param = param - LEARN_RATE * (first / first_fix) / (jnp.sqrt(second / second_fix) + ADAM_EPS)
    return param, first, second


def rows_dot(left, right):
    return lax.dot_general(left, right, (((0,), (0,)), ((), ())), preferred_element_type=F32)


def columns_dot(left, right):
    return lax.dot_general(left, right, (((1,), (1,)), ((), ())), preferred_element_type=F32)


def dot(left, right):
    return jnp.dot(left, right, preferred_element_type=F32)


def whole(shape):
    return pl.BlockSpec(shape, lambda i, core: (0,) * len(shape))


HBM = pl.BlockSpec(memory_space=pl.ANY)


def call(body, core, args, streamed, out_shape, flops, scratch=(), streamed_outs=()):
    outs = jax.tree.leaves(out_shape)
    moved = sum(a.size * a.dtype.itemsize for a in outs + list(args))
    out_specs = [
        HBM if index in streamed_outs else whole(out.shape) for index, out in enumerate(outs)
    ]
    single = not isinstance(out_shape, list)
    return pl.pallas_call(
        body,
        out_shape=out_shape,
        grid_spec=pltpu.PrefetchScalarGridSpec(
            num_scalar_prefetch=1,
            grid=(1,),
            in_specs=[
                HBM if index in streamed else whole(arg.shape) for index, arg in enumerate(args)
            ],
            out_specs=out_specs[0] if single else out_specs,
            scratch_shapes=list(scratch),
        ),
        compiler_params=pltpu.CompilerParams(vmem_limit_bytes=VMEM_LIMIT),
        cost_estimate=pl.CostEstimate(
            flops=flops // HINT, bytes_accessed=moved // HINT, transcendentals=0
        ),
    )(core, *args)


def started(pairs, sems):
    copies = [
        pltpu.make_async_copy(source, target, sems.at[index])
        for index, (source, target) in enumerate(pairs)
    ]
    for copy in copies:
        copy.start()
    return copies


def lanes_of(index, size=STEP):
    return pl.ds(index * size, size)


def frozen_back(core, cot, key_matrix, value_matrix, half, received=None, gain=None):
    tokens, kv = cot.shape[0], cot.shape[1] // 2
    steps = half // STEP
    own = received is not None

    def body(core_ref, cot_ref, key_ref, value_ref, *rest):
        if own:
            received_ref, gain_ref, *rest = rest
        out_ref, keys, values, out, key_sems, value_sems, out_sems, *rest = rest
        side = core_ref[0] if own else 1 - core_ref[0]
        base = pl.multiple_of(side * half, half)
        rows = [pl.ds(base + i * STEP, STEP) for i in range(steps)]
        copies = []
        for i in range(steps):
            pairs = [
                (key_ref.at[rows[i]], keys.at[lanes_of(i)], key_sems.at[i]),
                (value_ref.at[rows[i]], values.at[lanes_of(i)], value_sems.at[i]),
            ]
            if own:
                arrived, arrived_sems = rest
                pairs.append(
                    (
                        received_ref.at[:, lanes_of(i)],
                        arrived.at[:, lanes_of(i)],
                        arrived_sems.at[i],
                    )
                )
            copies.append([pltpu.make_async_copy(*pair) for pair in pairs])
            for copy in copies[i]:
                copy.start()
        leaving = []
        for i in range(steps):
            for copy in copies[i]:
                copy.wait()
            total = columns_dot(cot_ref[:, :kv], keys[lanes_of(i)])
            total += columns_dot(cot_ref[:, kv:], values[lanes_of(i)])
            if own:
                total = (total + arrived[:, lanes_of(i)].astype(F32)) * gain_ref[:, rows[i]]
            out[:, lanes_of(i)] = total.astype(BF16)
            leaving.append(
                pltpu.make_async_copy(
                    out.at[:, lanes_of(i)], out_ref.at[:, lanes_of(i)], out_sems.at[i]
                )
            )
            leaving[i].start()
        for copy in leaving:
            copy.wait()

    sems = pltpu.SemaphoreType.DMA((steps,))
    args = [cot, key_matrix, value_matrix]
    scratch = [
        pltpu.VMEM((half, kv), BF16),
        pltpu.VMEM((half, kv), BF16),
        pltpu.VMEM((tokens, half), BF16),
        sems,
        sems,
        sems,
    ]
    if own:
        args += [received, gain]
        scratch += [pltpu.VMEM((tokens, half), BF16), sems]
    return call(
        body,
        core,
        args,
        (1, 2, 3),
        jax.ShapeDtypeStruct((tokens, half), BF16),
        4 * tokens * half * kv,
        scratch,
        (0,),
    )


def normed_by_parity(core, x, rstd, gain, block):
    tokens, half = x.shape
    steps = half // STEP
    pairs = STEP // (2 * block)
    part = pairs * block

    def body(core_ref, x_ref, rstd_ref, gain_ref, kept_ref, given_ref, xs, kept, given, *sems):
        x_sems, kept_sems, given_sems = sems
        base = pl.multiple_of(core_ref[0] * half, half)
        copies = started(
            [(x_ref.at[:, lanes_of(i)], xs.at[:, lanes_of(i)]) for i in range(steps)], x_sems
        )
        rstd = rstd_ref[...]
        leaving = []
        for i in range(steps):
            copies[i].wait()
            for pair in range(pairs):
                for side in range(2):
                    start = i * STEP + (2 * pair + side) * block
                    normed = xs[:, start : start + block].astype(F32) * rstd
                    normed = (normed * gain_ref[:, pl.ds(base + start, block)]).astype(BF16)
                    out = lanes_of(i * pairs + pair, block)

                    @pl.when(core_ref[0] == side)
                    def _():
                        kept[:, out] = normed

                    @pl.when(core_ref[0] != side)
                    def _():
                        given[:, out] = normed

            for buffer, ref, out_sems in (
                (given, given_ref, given_sems),
                (kept, kept_ref, kept_sems),
            ):
                leaving.append(
                    pltpu.make_async_copy(
                        buffer.at[:, lanes_of(i, part)],
                        ref.at[:, lanes_of(i, part)],
                        out_sems.at[i],
                    )
                )
                leaving[-1].start()
        for copy in leaving:
            copy.wait()

    shape = jax.ShapeDtypeStruct((tokens, half // 2), BF16)
    sems = pltpu.SemaphoreType.DMA((steps,))
    return call(
        body,
        core,
        [x, rstd, gain],
        (0,),
        [shape, shape],
        tokens * half,
        [
            pltpu.VMEM((tokens, half), BF16),
            pltpu.VMEM((tokens, half // 2), BF16),
            pltpu.VMEM((tokens, half // 2), BF16),
            sems,
            sems,
            sems,
        ],
        (0, 1),
    )


def down_gradient(core, kept, taken, back, block):
    tokens, width = kept.shape
    count = width // block
    group = 4
    steps = count // group

    def body(core_ref, kept_ref, taken_ref, back_ref, out_ref, normed, out, in_sems, out_sems):
        copies = started(
            [(kept_ref, normed.at[0]), (taken_ref, normed.at[1])],
            in_sems,
        )
        turned = (ADAPTER_SCALING * back_ref[...].astype(F32)).T.astype(BF16)
        leaving = []
        for side in range(2):
            copies[side].wait()
            owner = core_ref[0] if side == 0 else 1 - core_ref[0]
            for step in range(steps):
                for index in range(step * group, (step + 1) * group):
                    piece = dot(turned, normed[side, :, index * block : (index + 1) * block])
                    out[side * count + index] = piece.astype(BF16)
                copy = pltpu.make_async_copy(
                    out.at[pl.ds(side * count + step * group, group)],
                    out_ref.at[pl.ds(owner * count + step * group, group)],
                    out_sems.at[side * steps + step],
                )
                copy.start()
                leaving.append(copy)
        for copy in leaving:
            copy.wait()

    return call(
        body,
        core,
        [kept, taken, back],
        (0, 1),
        jax.ShapeDtypeStruct((2 * count, COLUMNS, block), BF16),
        4 * tokens * width * COLUMNS,
        [
            pltpu.VMEM((2, tokens, width), BF16),
            pltpu.VMEM((2 * count, COLUMNS, block), BF16),
            pltpu.SemaphoreType.DMA((2,)),
            pltpu.SemaphoreType.DMA((2 * steps,)),
        ],
        (0,),
    )


def projected(core, x, x_other, rstd, gain, key_matrix, value_matrix, cot):
    tokens, half = x.shape
    kv = key_matrix.shape[1]
    steps = half // STEP

    def body(core_ref, x_ref, other_ref, rstd_ref, gain_ref, key_ref, value_ref, cot_ref, *rest):
        out_ref, sum_ref, xs, keys, values, x_sems, key_sems, value_sems = rest
        rows, copies = [], []
        for side, ref in enumerate((x_ref, other_ref)):
            base = core_ref[0] if side == 0 else 1 - core_ref[0]
            for i in range(steps):
                at = side * steps + i
                rows.append(pl.ds(pl.multiple_of(base * half + i * STEP, STEP), STEP))
                sources = [
                    (ref.at[:, lanes_of(i)], xs.at[:, lanes_of(at)], x_sems),
                    (key_ref.at[rows[at]], keys.at[lanes_of(at)], key_sems),
                    (value_ref.at[rows[at]], values.at[lanes_of(at)], value_sems),
                ]
                copies.append(
                    [pltpu.make_async_copy(a, b, sems.at[at]) for a, b, sems in sources]
                )
                for copy in copies[at]:
                    copy.start()
        rstd = rstd_ref[...]
        for at in range(2 * steps):
            for copy in copies[at]:
                copy.wait()
            normed = xs[:, lanes_of(at)].astype(F32) * rstd * gain_ref[:, rows[at]]
            normed = normed.astype(BF16)
            for lanes, matrix in ((slice(0, kv), keys), (slice(kv, 2 * kv), values)):
                product = dot(normed, matrix[lanes_of(at)])
                if at == 0:
                    out_ref[:, lanes] = product
                else:
                    out_ref[:, lanes] += product
        sum_ref[...] = jnp.sum(out_ref[...] * cot_ref[...].astype(F32), axis=1, keepdims=True)

    sems = pltpu.SemaphoreType.DMA((2 * steps,))
    return call(
        body,
        core,
        [x, x_other, rstd, gain, key_matrix, value_matrix, cot],
        (0, 1, 4, 5),
        [
            jax.ShapeDtypeStruct((tokens, 2 * kv), F32),
            jax.ShapeDtypeStruct((tokens, 1), F32),
        ],
        8 * tokens * half * kv,
        [
            pltpu.VMEM((tokens, 2 * half), BF16),
            pltpu.VMEM((2 * half, kv), BF16),
            pltpu.VMEM((2 * half, kv), BF16),
            sems,
            sems,
            sems,
        ],
    )


def low_rank_down(core, x, rstd, gain, factors):
    tokens, half = x.shape
    steps = half // STEP

    def body(core_ref, x_ref, rstd_ref, gain_ref, factors_ref, out_ref, xs, ours, x_sems, sems):
        base = pl.multiple_of(core_ref[0] * half, half)
        copies = []
        for i in range(steps):
            copies.append(
                [
                    pltpu.make_async_copy(
                        x_ref.at[:, lanes_of(i)], xs.at[:, lanes_of(i)], x_sems.at[i]
                    ),
                    pltpu.make_async_copy(
                        factors_ref.at[pl.ds(base + i * STEP, STEP), :COLUMNS],
                        ours.at[lanes_of(i)],
                        sems.at[i],
                    ),
                ]
            )
            for copy in copies[i]:
                copy.start()
        rstd = rstd_ref[...]
        for i in range(steps):
            for copy in copies[i]:
                copy.wait()
            normed = xs[:, lanes_of(i)].astype(F32) * rstd
            normed = (normed * gain_ref[:, pl.ds(base + i * STEP, STEP)]).astype(BF16)
            product = dot(normed, ours[lanes_of(i)])
            if i == 0:
                out_ref[...] = product
            else:
                out_ref[...] += product

    sems = pltpu.SemaphoreType.DMA((steps,))
    return call(
        body,
        core,
        [x, rstd, gain, factors],
        (0, 3),
        jax.ShapeDtypeStruct((tokens, COLUMNS), F32),
        2 * tokens * half * COLUMNS,
        [
            pltpu.VMEM((tokens, half), BF16),
            pltpu.VMEM((half, COLUMNS), BF16),
            sems,
            sems,
        ],
    )


def masked(value, jobs):
    column = lax.broadcasted_iota(jnp.int32, value.shape, 1)
    return jnp.where(jobs == (column & (FEATURE_WIDTH - 1)) // RANK, value, 0.0)


def back_product(scalars, cot, ups):
    tokens, kv = cot.shape[0], cot.shape[1] // 2
    rows = ups[0].shape[1]

    def body(scalars_ref, cot_ref, *rest):
        up_refs, (out_ref, up_ref, ordered) = rest[:SIDE], rest[SIDE:]
        for down, ref in enumerate(up_refs):
            z = lax.rem(scalars_ref[1] + SIDE - down, SIDE)
            for left in range(SIDE):
                y = lax.rem(scalars_ref[2] + SIDE - left, SIDE)
                start = pl.multiple_of((z * SIDE + y) * rows, rows)
                ordered[pl.ds(start, rows), :] = ref[left].astype(F32)
        up_ref[...] = ordered[...].astype(BF16)
        for side in range(2):
            lanes = pl.ds(side * kv, kv)
            picked = columns_dot(cot_ref[:, lanes], up_ref[:, lanes])
            out_ref[:, side * FEATURE_WIDTH : (side + 1) * FEATURE_WIDTH] = picked

    return call(
        body,
        scalars,
        [cot, *ups],
        (),
        [
            jax.ShapeDtypeStruct((tokens, COLUMNS), F32),
            jax.ShapeDtypeStruct((FEATURE_WIDTH, 2 * kv), BF16),
        ],
        4 * tokens * kv * FEATURE_WIDTH,
        [pltpu.VMEM((FEATURE_WIDTH, 2 * kv), F32)],
    )


def up_gradient(core, mine, other, jobs, cot, back):
    tokens, kv = cot.shape[0], cot.shape[1] // 2

    def body(core_ref, mine_ref, other_ref, jobs_ref, cot_ref, back_ref, *outs):
        low_ref, out_ref, sum_ref = outs
        total = masked(mine_ref[...] + other_ref[...], jobs_ref[...])
        sum_ref[...] = ADAPTER_SCALING * jnp.sum(
            total * back_ref[...].astype(F32), axis=1, keepdims=True
        )
        low = total.astype(BF16)
        low_ref[...] = low
        for side in range(2):
            lanes = lanes_of(side, kv)
            picked = low[:, side * FEATURE_WIDTH : (side + 1) * FEATURE_WIDTH]
            out_ref[:, lanes] = (ADAPTER_SCALING * rows_dot(picked, cot_ref[:, lanes])).astype(BF16)

    return call(
        body,
        core,
        [mine, other, jobs, cot, back],
        (),
        [
            jax.ShapeDtypeStruct((tokens, COLUMNS), BF16),
            jax.ShapeDtypeStruct((FEATURE_WIDTH, 2 * kv), BF16),
            jax.ShapeDtypeStruct((tokens, 1), F32),
        ],
        4 * tokens * kv * FEATURE_WIDTH,
    )


def with_low_rank(core, frozen, low, up):
    tokens, kv = frozen.shape[0], frozen.shape[1] // 2

    def body(core_ref, frozen_ref, low_ref, up_ref, out_ref):
        for side in range(2):
            lanes = lanes_of(side, kv)
            picked = low_ref[:, side * FEATURE_WIDTH : (side + 1) * FEATURE_WIDTH]
            total = frozen_ref[:, lanes] + ADAPTER_SCALING * dot(picked, up_ref[:, lanes])
            out_ref[:, lanes] = total.astype(BF16)

    return call(
        body,
        core,
        [frozen, low, up],
        (),
        jax.ShapeDtypeStruct(frozen.shape, BF16),
        4 * tokens * kv * FEATURE_WIDTH,
    )


def norm_backward(core, scaled, back, factors, gain, x, rstd, mean):
    tokens, half = x.shape
    steps = half // STEP

    def body(core_ref, scaled_ref, back_ref, factors_ref, gain_ref, x_ref, *rest):
        rstd_ref, mean_ref, out_ref, ins, ours, xs, out, in_sems, sems, x_sems, out_sems = rest
        base = pl.multiple_of(core_ref[0] * half, half)
        rows = [pl.ds(base + i * STEP, STEP) for i in range(steps)]
        copies = []
        for i in range(steps):
            lanes = lanes_of(i)
            sources = [
                (factors_ref.at[rows[i], COLUMNS:], ours.at[lanes], sems),
                (x_ref.at[:, lanes], xs.at[:, lanes], x_sems),
                (scaled_ref.at[:, lanes], ins.at[:, lanes], in_sems),
            ]
            copies.append([pltpu.make_async_copy(a, b, c.at[i]) for a, b, c in sources])
            for copy in copies[i]:
                copy.start()
        back = back_ref[...]
        rstd = rstd_ref[...]
        shift = rstd * rstd * mean_ref[...]
        leaving = []
        for i in range(steps):
            lanes = lanes_of(i)
            for copy in copies[i]:
                copy.wait()
            low = columns_dot(back, ours[lanes])
            total = ins[:, lanes].astype(F32) + (ADAPTER_SCALING * gain_ref[:, rows[i]]) * low
            out[:, lanes] = (rstd * total - xs[:, lanes].astype(F32) * shift).astype(BF16)
            leaving.append(
                pltpu.make_async_copy(out.at[:, lanes], out_ref.at[:, lanes], out_sems.at[i])
            )
            leaving[i].start()
        for copy in leaving:
            copy.wait()

    sems = pltpu.SemaphoreType.DMA((steps,))
    strip = pltpu.VMEM((tokens, half), BF16)
    return call(
        body,
        core,
        [scaled, back, factors, gain, x, rstd, mean],
        (0, 2, 4),
        jax.ShapeDtypeStruct((tokens, half), BF16),
        2 * tokens * half * COLUMNS,
        [strip, pltpu.VMEM((half, COLUMNS), BF16), strip, strip, sems, sems, sems, sems],
        (0,),
    )


def summed(core, pieces):
    count, rows, columns = pieces.shape
    steps = 4
    part = rows // steps

    def body(core_ref, pieces_ref, out_ref, held, sems):
        copies = started(
            [
                (pieces_ref.at[:, lanes_of(i, part)], held.at[:, lanes_of(i, part)])
                for i in range(steps)
            ],
            sems,
        )
        for i in range(steps):
            copies[i].wait()
            total = jnp.sum(held[:, lanes_of(i, part)].astype(F32), axis=0)
            out_ref[lanes_of(i, part)] = total.astype(BF16)

    return call(
        body,
        core,
        [pieces],
        (0,),
        jax.ShapeDtypeStruct((rows, columns), BF16),
        pieces.size,
        [pltpu.VMEM(pieces.shape, BF16), pltpu.SemaphoreType.DMA((steps,))],
    )


def down_optimizer(scalars, params, second, grad, totals):
    rows, columns = grad.shape

    def body(scalars_ref, params_ref, second_ref, grad_ref, totals_ref, new_ref, chosen_ref, turned):
        grad = grad_ref[...].astype(F32).T / totals_ref[...]
        new = adam_update(params_ref[0], params_ref[1], second_ref[...], grad)
        job = pl.multiple_of(scalars_ref[1] * RANK, RANK)
        for index, value in enumerate(new):
            new_ref[index] = value
            turned[...] = value.T
            for side in range(2):
                picked = turned[pl.ds(side * FEATURE_WIDTH + job, RANK), :]
                chosen_ref[index, side * RANK : (side + 1) * RANK] = picked

    return call(
        body,
        scalars,
        [params, second, grad, totals],
        (),
        [
            jax.ShapeDtypeStruct((3, rows, columns), F32),
            jax.ShapeDtypeStruct((3, 2 * RANK, rows), F32),
        ],
        20 * rows * columns,
        [pltpu.VMEM((columns, rows), F32)],
    )


def local(
    carried,
    norm_gain,
    frozen_key_matrix,
    frozen_value_matrix,
    adapter_params,
    adapter_second,
    right_params,
    right_second,
    row_jobs,
    job_tokens,
    finishing,
    cotangent,
):
    n_data = lax.axis_size("dp")
    core_index = lax.axis_index("tensor")
    core = core_index[None].astype(jnp.int32)
    place = lax.axis_index("dp")
    x_here = carried[0]
    tokens, half = x_here.shape
    width = 2 * half
    block = adapter_params.shape[2]
    kv = frozen_key_matrix.shape[2]
    gain = norm_gain
    key_matrix, value_matrix = frozen_key_matrix[0], frozen_value_matrix[0]
    cot = cotangent[0].reshape(tokens, 2 * kv)
    jobs = row_jobs[0][:, None]

    factors = adapter_params[0, 0].astype(BF16)
    factors_next = shifted(factors, "section", -1)
    x_in = shifted(x_here, "section", 1)
    gain_next = shifted(gain, "section", -1)
    both = lax.all_gather(
        jnp.concatenate([factors, factors_next], axis=1), ("dp", "tensor"), axis=0, tiled=True
    )

    up_here = right_params[0, 0].astype(BF16).reshape(-1, 2 * kv)
    rows_local = up_here.shape[0]
    up_row = jnp.stack([up_here] + [shifted_y(up_here, step) for step in range(1, SIDE)])
    ups = [up_row] + [shifted_z(up_row, step) for step in range(1, SIDE)]
    spot = jnp.stack([core_index, place // SIDE, place % SIDE]).astype(jnp.int32)

    leaving = frozen_back(after(core, up_row), cot, key_matrix, value_matrix, half)
    received = swapped(leaving)

    back_part, up = back_product(after(spot, leaving), cot, ups)
    back = masked(back_part + swapped(back_part), jobs).astype(BF16)
    back_next = shifted(back, "section", -1)

    scaled = frozen_back(
        after(core, back), cot, key_matrix, value_matrix, half, received, gain
    )
    scaled_next = shifted(scaled, "section", -1)

    x_wide = x_here.astype(F32)
    squares = jnp.sum(x_wide * x_wide, axis=1, keepdims=True)
    rstd = lax.rsqrt((squares + swapped(squares)) / width + 1e-05)
    rstd_in = shifted(rstd, "section", 1)
    kept, given = normed_by_parity(after(core, scaled), x_here, rstd, gain_next, block)
    down_piece = down_gradient(core, kept, swapped(given), back_next, block)
    down_pieces = lax.all_to_all(down_piece, "dp", 0, 0, tiled=True)

    x_in = after(x_in, down_piece)
    frozen, products = projected(
        core, x_in, swapped(x_in), rstd_in, gain, key_matrix, value_matrix, cot
    )
    low_part = low_rank_down(after(core, frozen), x_in, rstd_in, gain, both)
    low, up_piece, low_products = up_gradient(
        core, low_part, swapped(low_part), jobs, cot, back
    )
    up_pieces = up_piece.reshape(n_data, rows_local, 2 * kv)
    up_pieces = lax.all_to_all(up_pieces, "dp", 0, 0, tiled=True)
    mean = shifted((products + swapped(products) + low_products) / width, "section", -1)
    down_sum = summed(after(core, up_piece), down_pieces)
    kv_out = with_low_rank(after(core, down_sum), frozen, low, up)
    down_sum = shifted(down_sum, "section", 1)

    input_grad = norm_backward(
        after(core, kv_out), scaled_next, back_next, both, gain_next, x_here, rstd, mean
    )
    kv_out = kv_out.reshape(1, tokens, 2, kv)
    up_sum = jnp.sum(up_pieces.astype(F32), axis=0).reshape(rows_local, 2, kv)

    job_ids = jnp.arange(JOBS, dtype=jnp.int32)
    counts = job_tokens.astype(F32)
    col_job = jnp.arange(COLUMNS, dtype=jnp.int32) % FEATURE_WIDTH // RANK
    column_total = jnp.sum(
        jnp.where(col_job[:, None] == job_ids[None, :], counts[None, :], 0.0), axis=1
    )
    row_job = (place * rows_local + jnp.arange(rows_local, dtype=jnp.int32)) // RANK
    row_count = jnp.sum(
        jnp.where(row_job[:, None] == job_ids[None, :], counts[None, :], 0.0), axis=1
    )
    scalars = jnp.concatenate([after(core, input_grad), finishing.astype(jnp.int32)])
    new_a, chosen = down_optimizer(
        scalars, adapter_params[0], adapter_second[0], down_sum, column_total[None, :]
    )
    new_b = jnp.stack(
        adam_update(
            right_params[0, 0],
            right_params[0, 1],
            right_second[0],
            up_sum / row_count[:, None, None],
        )
    )
    other = swapped(chosen)
    own = core_index == 0
    checkpoint = jnp.concatenate(
        [jnp.where(own, chosen, other), jnp.where(own, other, chosen)], axis=2
    )[None]
    return (kv_out, input_grad[None], new_a[None], new_b[None], checkpoint)


def solution(mesh):
    return jax.shard_map(
        local,
        mesh=mesh,
        in_specs=(
            P("section", "dp", "tensor"),
            P("section", None),
            P("section", None, "tensor"),
            P("section", None, "tensor"),
            P("section", None, ("dp", "tensor"), None),
            P("section", ("dp", "tensor"), None),
            P("section", None, "dp", None, "tensor"),
            P("section", "dp", None, "tensor"),
            P("section", "dp"),
            P(),
            P("section"),
            P("section", "dp", None, "tensor"),
        ),
        out_specs=(
            P("section", "dp", None, "tensor"),
            P("section", "dp", "tensor"),
            P("section", None, ("dp", "tensor"), None),
            P("section", None, "dp", None, "tensor"),
            P("section", None, None, "dp"),
        ),
        check_vma=False,
    )
```

```python
import jax
import jax.numpy as jnp
from jax import lax
from jax.experimental import pallas as pl
from jax.experimental.pallas import tpu as pltpu
from jax.sharding import PartitionSpec as P

JOBS = 8
RANK = 16
ADAM_STEP = 10
ADAPTER_SCALING = 2.0
BETA_ONE = 0.9
BETA_TWO = 0.999
ADAM_EPS = 1e-08
LEARN_RATE = 0.01

FEATURE_WIDTH = JOBS * RANK
COLUMNS = 2 * FEATURE_WIDTH
STEP = 1024
VMEM_LIMIT = 54 * 1024 * 1024
FULL_LIMIT = 60 * 1024 * 1024
SMALL_LIMIT = 24 * 1024 * 1024
HINT = 16
CHUNKS = 2
PARTS = 2

F32 = jnp.float32
BF16 = jnp.bfloat16


def shifted(value, axis, steps):
    count = lax.axis_size(axis)
    pairs = [(source, (source + steps) % count) for source in range(count)]
    return lax.ppermute(value, axis, pairs)


def swapped(value):
    return shifted(value, "tensor", 1)


def after(value, *others):
    return lax.optimization_barrier((value,) + others)[0]


def adam_update(param, first, second, grad):
    first = BETA_ONE * first + (1.0 - BETA_ONE) * grad
    second = BETA_TWO * second + (1.0 - BETA_TWO) * grad * grad
    first_fix = 1.0 - BETA_ONE**ADAM_STEP
    second_fix = 1.0 - BETA_TWO**ADAM_STEP
    param = param - LEARN_RATE * (first / first_fix) / (jnp.sqrt(second / second_fix) + ADAM_EPS)
    return param, first, second


def rows_dot(left, right):
    return lax.dot_general(left, right, (((0,), (0,)), ((), ())), preferred_element_type=F32)


def columns_dot(left, right):
    return lax.dot_general(left, right, (((1,), (1,)), ((), ())), preferred_element_type=F32)


def dot(left, right):
    return jnp.dot(left, right, preferred_element_type=F32)


def whole(shape):
    return pl.BlockSpec(shape, lambda i, core: (0,) * len(shape))


HBM = pl.BlockSpec(memory_space=pl.ANY)


def call(
    body, core, args, streamed, out_shape, flops, scratch=(), streamed_outs=(), limit=SMALL_LIMIT
):
    outs = jax.tree.leaves(out_shape)
    moved = sum(a.size * a.dtype.itemsize for a in outs + list(args))
    out_specs = [
        HBM if index in streamed_outs else whole(out.shape) for index, out in enumerate(outs)
    ]
    single = not isinstance(out_shape, list)
    return pl.pallas_call(
        body,
        out_shape=out_shape,
        grid_spec=pltpu.PrefetchScalarGridSpec(
            num_scalar_prefetch=1,
            grid=(1,),
            in_specs=[
                HBM if index in streamed else whole(arg.shape) for index, arg in enumerate(args)
            ],
            out_specs=out_specs[0] if single else out_specs,
            scratch_shapes=list(scratch),
        ),
        compiler_params=pltpu.CompilerParams(vmem_limit_bytes=limit),
        cost_estimate=pl.CostEstimate(
            flops=flops // HINT, bytes_accessed=moved // HINT, transcendentals=0
        ),
    )(core, *args)


def started(pairs, sems):
    copies = [
        pltpu.make_async_copy(source, target, sems.at[index])
        for index, (source, target) in enumerate(pairs)
    ]
    for copy in copies:
        copy.start()
    return copies


def lanes_of(index, size=STEP):
    return pl.ds(index * size, size)


def frozen_back(core, cot, key_matrix, value_matrix, half, received=None, gain=None):
    tokens, kv = cot.shape[0], cot.shape[1] // 2
    steps = half // STEP
    own = received is not None
    parts = CHUNKS
    within = steps // parts

    def body(core_ref, cot_ref, key_ref, value_ref, *rest):
        if own:
            received_refs, (gain_ref, *rest) = rest[:parts], rest[parts:]
            out_refs, rest = rest[:1], rest[1:]
        else:
            out_refs, rest = rest[:parts], rest[parts:]
        keys, values, out, key_sems, value_sems, out_sems, *rest = rest
        side = core_ref[0] if own else 1 - core_ref[0]
        base = pl.multiple_of(side * half, half)
        rows = [pl.ds(base + i * STEP, STEP) for i in range(steps)]
        copies = []
        for i in range(steps):
            pairs = [
                (key_ref.at[rows[i]], keys.at[lanes_of(i)], key_sems.at[i]),
                (value_ref.at[rows[i]], values.at[lanes_of(i)], value_sems.at[i]),
            ]
            if own:
                arrived, arrived_sems = rest
                pairs.append(
                    (
                        received_refs[i // within].at[:, lanes_of(i % within)],
                        arrived.at[:, lanes_of(i)],
                        arrived_sems.at[i],
                    )
                )
            copies.append([pltpu.make_async_copy(*pair) for pair in pairs])
            for copy in copies[i]:
                copy.start()
        leaving = []
        for i in range(steps):
            for copy in copies[i]:
                copy.wait()
            total = columns_dot(cot_ref[:, :kv], keys[lanes_of(i)])
            total += columns_dot(cot_ref[:, kv:], values[lanes_of(i)])
            if own:
                total = (total + arrived[:, lanes_of(i)].astype(F32)) * gain_ref[:, rows[i]]
            out[:, lanes_of(i)] = total.astype(BF16)
            if own:
                target = out_refs[0].at[:, lanes_of(i)]
            else:
                target = out_refs[i // within].at[:, lanes_of(i % within)]
            leaving.append(pltpu.make_async_copy(out.at[:, lanes_of(i)], target, out_sems.at[i]))
            leaving[i].start()
        for copy in leaving:
            copy.wait()

    sems = pltpu.SemaphoreType.DMA((steps,))
    args = [cot, key_matrix, value_matrix]
    scratch = [
        pltpu.VMEM((half, kv), BF16),
        pltpu.VMEM((half, kv), BF16),
        pltpu.VMEM((tokens, half), BF16),
        sems,
        sems,
        sems,
    ]
    if own:
        args += [*received, gain]
        scratch += [pltpu.VMEM((tokens, half), BF16), sems]
    piece = jax.ShapeDtypeStruct((tokens, half // parts), BF16)
    return call(
        body,
        core,
        args,
        (1, 2) + tuple(range(3, 3 + parts)) * own,
        jax.ShapeDtypeStruct((tokens, half), BF16) if own else [piece] * parts,
        4 * tokens * half * kv,
        scratch,
        tuple(range(1 if own else parts)),
        VMEM_LIMIT,
    )


def normed_by_parity(core, x, rstd, gain, block):
    tokens, half = x.shape
    steps = half // STEP
    pairs = STEP // (2 * block)
    part = pairs * block

    def body(core_ref, x_ref, rstd_ref, gain_ref, kept_ref, given_ref, xs, kept, given, *sems):
        x_sems, kept_sems, given_sems = sems
        base = pl.multiple_of(core_ref[0] * half, half)
        copies = started(
            [(x_ref.at[:, lanes_of(i)], xs.at[:, lanes_of(i)]) for i in range(steps)], x_sems
        )
        rstd = rstd_ref[...]
        leaving = []
        for i in range(steps):
            copies[i].wait()
            for pair in range(pairs):
                for side in range(2):
                    start = i * STEP + (2 * pair + side) * block
                    normed = xs[:, start : start + block].astype(F32) * rstd
                    normed = (normed * gain_ref[:, pl.ds(base + start, block)]).astype(BF16)
                    out = lanes_of(i * pairs + pair, block)

                    @pl.when(core_ref[0] == side)
                    def _():
                        kept[:, out] = normed

                    @pl.when(core_ref[0] != side)
                    def _():
                        given[:, out] = normed

            for buffer, ref, out_sems in (
                (given, given_ref, given_sems),
                (kept, kept_ref, kept_sems),
            ):
                leaving.append(
                    pltpu.make_async_copy(
                        buffer.at[:, lanes_of(i, part)],
                        ref.at[:, lanes_of(i, part)],
                        out_sems.at[i],
                    )
                )
                leaving[-1].start()
        for copy in leaving:
            copy.wait()

    shape = jax.ShapeDtypeStruct((tokens, half // 2), BF16)
    sems = pltpu.SemaphoreType.DMA((steps,))
    return call(
        body,
        core,
        [x, rstd, gain],
        (0,),
        [shape, shape],
        tokens * half,
        [
            pltpu.VMEM((tokens, half), BF16),
            pltpu.VMEM((tokens, half // 2), BF16),
            pltpu.VMEM((tokens, half // 2), BF16),
            sems,
            sems,
            sems,
        ],
        (0, 1),
    )


def down_gradient(core, kept, taken, back, block):
    tokens, width = kept.shape
    count = width // block
    group = 4
    steps = count // group

    def body(core_ref, kept_ref, taken_ref, back_ref, out_ref, normed, out, in_sems, out_sems):
        copies = started(
            [(kept_ref, normed.at[0]), (taken_ref, normed.at[1])],
            in_sems,
        )
        turned = (ADAPTER_SCALING * back_ref[...].astype(F32)).T.astype(BF16)
        leaving = []
        for side in range(2):
            copies[side].wait()
            owner = core_ref[0] if side == 0 else 1 - core_ref[0]
            for step in range(steps):
                for index in range(step * group, (step + 1) * group):
                    piece = dot(turned, normed[side, :, index * block : (index + 1) * block])
                    out[side * count + index] = piece.astype(BF16)
                copy = pltpu.make_async_copy(
                    out.at[pl.ds(side * count + step * group, group)],
                    out_ref.at[pl.ds(owner * count + step * group, group)],
                    out_sems.at[side * steps + step],
                )
                copy.start()
                leaving.append(copy)
        for copy in leaving:
            copy.wait()

    return call(
        body,
        core,
        [kept, taken, back],
        (0, 1),
        jax.ShapeDtypeStruct((2 * count, COLUMNS, block), BF16),
        4 * tokens * width * COLUMNS,
        [
            pltpu.VMEM((2, tokens, width), BF16),
            pltpu.VMEM((2 * count, COLUMNS, block), BF16),
            pltpu.SemaphoreType.DMA((2,)),
            pltpu.SemaphoreType.DMA((2 * steps,)),
        ],
        (0,),
    )


def projected(core, own, other, start, half, gain, key_matrix, value_matrix, cot, before=None):
    tokens, part = own.shape
    kv = key_matrix.shape[1]
    within = part // STEP
    steps = 2 * within
    last = before is not None

    def body(core_ref, own_ref, other_ref, gain_ref, key_ref, value_ref, *rest):
        if last:
            cot_ref, before_ref, sums_before_ref, *rest = rest
        out_ref, sums_ref, *rest = rest
        held, keys, values, x_sems, key_sems, value_sems = rest
        rows, copies = [], []
        for i in range(steps):
            ref, side = (own_ref, core_ref[0]) if i < within else (other_ref, 1 - core_ref[0])
            first = side * half + start + i % within * STEP
            rows.append(pl.ds(pl.multiple_of(first, STEP), STEP))
            sources = [
                (ref.at[:, lanes_of(i % within)], held.at[:, lanes_of(i)], x_sems),
                (key_ref.at[rows[i]], keys.at[lanes_of(i)], key_sems),
                (value_ref.at[rows[i]], values.at[lanes_of(i)], value_sems),
            ]
            copies.append([pltpu.make_async_copy(a, b, sems.at[i]) for a, b, sems in sources])
            for copy in copies[i]:
                copy.start()
        for i in range(steps):
            for copy in copies[i]:
                copy.wait()
            wide = held[:, lanes_of(i)].astype(F32)
            if i < within:
                square = jnp.sum(wide * wide, axis=1, keepdims=True)
                squares = square if i == 0 else squares + square
            scaled = (wide * gain_ref[:, rows[i]]).astype(BF16)
            for lanes, matrix in ((slice(0, kv), keys), (slice(kv, 2 * kv), values)):
                product = dot(scaled, matrix[lanes_of(i)])
                if i > 0:
                    out_ref[:, lanes] += product
                elif last:
                    out_ref[:, lanes] = before_ref[:, lanes] + product
                else:
                    out_ref[:, lanes] = product
        sums_ref[...] = jnp.broadcast_to(squares, sums_ref.shape)
        if last:
            products = jnp.sum(out_ref[...] * cot_ref[...].astype(F32), axis=1, keepdims=True)
            lane = lax.broadcasted_iota(jnp.int32, sums_ref.shape, 1)
            sums_ref[...] = jnp.where(lane == 0, squares + sums_before_ref[...], products)

    sems = pltpu.SemaphoreType.DMA((steps,))
    total = jax.ShapeDtypeStruct((tokens, 2 * kv), F32)
    return call(
        body,
        core,
        [own, other, gain, key_matrix, value_matrix] + ([cot, *before] if last else []),
        (0, 1, 3, 4),
        [total, jax.ShapeDtypeStruct((tokens, 128), F32)],
        8 * tokens * part * kv,
        [
            pltpu.VMEM((tokens, 2 * part), BF16),
            pltpu.VMEM((2 * part, kv), BF16),
            pltpu.VMEM((2 * part, kv), BF16),
            sems,
            sems,
            sems,
        ],
        limit=VMEM_LIMIT,
    )


def low_rank_down(core, xs, gain, factors):
    parts = len(xs)
    tokens, part = xs[0].shape
    half = parts * part
    within = part // STEP
    steps = half // STEP

    def body(core_ref, *rest):
        x_refs, rest = rest[:parts], rest[parts:]
        gain_ref, factors_ref, out_ref, held, ours, x_sems, sems = rest
        base = pl.multiple_of(core_ref[0] * half, half)
        copies = []
        for i in range(steps):
            copies.append(
                [
                    pltpu.make_async_copy(
                        x_refs[i // within].at[:, lanes_of(i % within)],
                        held.at[:, lanes_of(i)],
                        x_sems.at[i],
                    ),
                    pltpu.make_async_copy(
                        factors_ref.at[pl.ds(base + i * STEP, STEP), :COLUMNS],
                        ours.at[lanes_of(i)],
                        sems.at[i],
                    ),
                ]
            )
            for copy in copies[i]:
                copy.start()
        for i in range(steps):
            for copy in copies[i]:
                copy.wait()
            scaled = held[:, lanes_of(i)].astype(F32) * gain_ref[:, pl.ds(base + i * STEP, STEP)]
            product = dot(scaled.astype(BF16), ours[lanes_of(i)])
            if i == 0:
                out_ref[...] = product
            else:
                out_ref[...] += product

    sems = pltpu.SemaphoreType.DMA((steps,))
    return call(
        body,
        core,
        [*xs, gain, factors],
        tuple(range(parts)) + (parts + 1,),
        jax.ShapeDtypeStruct((tokens, COLUMNS), F32),
        2 * tokens * half * COLUMNS,
        [
            pltpu.VMEM((tokens, half), BF16),
            pltpu.VMEM((half, COLUMNS), BF16),
            sems,
            sems,
        ],
        limit=VMEM_LIMIT,
    )


def masked(value, jobs):
    column = lax.broadcasted_iota(jnp.int32, value.shape, 1)
    return jnp.where(jobs == (column & (FEATURE_WIDTH - 1)) // RANK, value, 0.0)


def back_product(core, cot, up):
    tokens, kv = cot.shape[0], cot.shape[1] // 2

    def body(core_ref, cot_ref, up_ref, out_ref):
        for side in range(2):
            lanes = lanes_of(side, kv)
            picked = columns_dot(cot_ref[:, lanes], up_ref[:, lanes])
            out_ref[:, side * FEATURE_WIDTH : (side + 1) * FEATURE_WIDTH] = picked

    return call(
        body,
        core,
        [cot, up],
        (),
        jax.ShapeDtypeStruct((tokens, COLUMNS), F32),
        4 * tokens * kv * FEATURE_WIDTH,
    )


def up_gradient(core, mine, other, jobs, cot, back, sums, other_sums, width):
    tokens, kv = cot.shape[0], cot.shape[1] // 2

    def body(core_ref, mine_ref, other_ref, jobs_ref, cot_ref, back_ref, *rest):
        sums_ref, other_sums_ref, low_ref, out_ref, rstd_ref, mean_ref = rest
        sums = sums_ref[...] + other_sums_ref[...]
        rstd = lax.rsqrt(sums[:, :1] / width + 1e-05)
        rstd_ref[...] = rstd
        total = masked((mine_ref[...] + other_ref[...]) * rstd, jobs_ref[...])
        low_products = jnp.sum(total * back_ref[...].astype(F32), axis=1, keepdims=True)
        mean_ref[...] = (sums[:, 1:2] * rstd + ADAPTER_SCALING * low_products) / width
        low = total.astype(BF16)
        low_ref[...] = low
        for side in range(2):
            lanes = lanes_of(side, kv)
            picked = low[:, side * FEATURE_WIDTH : (side + 1) * FEATURE_WIDTH]
            out_ref[:, lanes] = (ADAPTER_SCALING * rows_dot(picked, cot_ref[:, lanes])).astype(BF16)

    column = jax.ShapeDtypeStruct((tokens, 1), F32)
    return call(
        body,
        core,
        [mine, other, jobs, cot, back, sums, other_sums],
        (),
        [
            jax.ShapeDtypeStruct((tokens, COLUMNS), BF16),
            jax.ShapeDtypeStruct((FEATURE_WIDTH, 2 * kv), BF16),
            column,
            column,
        ],
        4 * tokens * kv * FEATURE_WIDTH,
        limit=FULL_LIMIT,
    )


def with_low_rank(core, frozen, low, up, rstd):
    tokens, kv = frozen.shape[0], frozen.shape[1] // 2

    def body(core_ref, frozen_ref, low_ref, up_ref, rstd_ref, out_ref):
        for side in range(2):
            lanes = lanes_of(side, kv)
            picked = low_ref[:, side * FEATURE_WIDTH : (side + 1) * FEATURE_WIDTH]
            total = frozen_ref[:, lanes] * rstd_ref[...]
            total += ADAPTER_SCALING * dot(picked, up_ref[:, lanes])
            out_ref[:, lanes] = total.astype(BF16)

    return call(
        body,
        core,
        [frozen, low, up, rstd],
        (),
        jax.ShapeDtypeStruct(frozen.shape, BF16),
        4 * tokens * kv * FEATURE_WIDTH,
    )


def norm_backward(core, scaled, back, factors, gain, x, rstd, mean):
    tokens, half = x.shape
    steps = half // STEP

    def body(core_ref, scaled_ref, back_ref, factors_ref, gain_ref, x_ref, *rest):
        rstd_ref, mean_ref, out_ref, ins, ours, xs, out, in_sems, sems, x_sems, out_sems = rest
        base = pl.multiple_of(core_ref[0] * half, half)
        rows = [pl.ds(base + i * STEP, STEP) for i in range(steps)]
        copies = []
        for i in range(steps):
            lanes = lanes_of(i)
            sources = [
                (factors_ref.at[rows[i], COLUMNS:], ours.at[lanes], sems),
                (x_ref.at[:, lanes], xs.at[:, lanes], x_sems),
                (scaled_ref.at[:, lanes], ins.at[:, lanes], in_sems),
            ]
            copies.append([pltpu.make_async_copy(a, b, c.at[i]) for a, b, c in sources])
            for copy in copies[i]:
                copy.start()
        back = back_ref[...]
        rstd = rstd_ref[...]
        shift = rstd * rstd * mean_ref[...]
        leaving = []
        for i in range(steps):
            lanes = lanes_of(i)
            for copy in copies[i]:
                copy.wait()
            low = columns_dot(back, ours[lanes])
            total = ins[:, lanes].astype(F32) + (ADAPTER_SCALING * gain_ref[:, rows[i]]) * low
            out[:, lanes] = (rstd * total - xs[:, lanes].astype(F32) * shift).astype(BF16)
            leaving.append(
                pltpu.make_async_copy(out.at[:, lanes], out_ref.at[:, lanes], out_sems.at[i])
            )
            leaving[i].start()
        for copy in leaving:
            copy.wait()

    sems = pltpu.SemaphoreType.DMA((steps,))
    strip = pltpu.VMEM((tokens, half), BF16)
    return call(
        body,
        core,
        [scaled, back, factors, gain, x, rstd, mean],
        (0, 2, 4),
        jax.ShapeDtypeStruct((tokens, half), BF16),
        2 * tokens * half * COLUMNS,
        [strip, pltpu.VMEM((half, COLUMNS), BF16), strip, strip, sems, sems, sems, sems],
        (0,),
        VMEM_LIMIT,
    )


def summed(core, pieces):
    count, rows, columns = pieces.shape
    steps = 4
    part = rows // steps

    def body(core_ref, pieces_ref, out_ref, held, sems):
        copies = started(
            [
                (pieces_ref.at[:, lanes_of(i, part)], held.at[:, lanes_of(i, part)])
                for i in range(steps)
            ],
            sems,
        )
        for i in range(steps):
            copies[i].wait()
            total = jnp.sum(held[:, lanes_of(i, part)].astype(F32), axis=0)
            out_ref[lanes_of(i, part)] = total.astype(BF16)

    return call(
        body,
        core,
        [pieces],
        (0,),
        jax.ShapeDtypeStruct((rows, columns), BF16),
        pieces.size,
        [pltpu.VMEM(pieces.shape, BF16), pltpu.SemaphoreType.DMA((steps,))],
    )


def down_optimizer(scalars, params, second, grad, totals):
    rows, columns = grad.shape

    def body(scalars_ref, params_ref, second_ref, grad_ref, totals_ref, new_ref, chosen_ref, turned):
        grad = grad_ref[...].astype(F32).T / totals_ref[...]
        new = adam_update(params_ref[0], params_ref[1], second_ref[...], grad)
        job = pl.multiple_of(scalars_ref[1] * RANK, RANK)
        for index, value in enumerate(new):
            new_ref[index] = value
            turned[...] = value.T
            for side in range(2):
                picked = turned[pl.ds(side * FEATURE_WIDTH + job, RANK), :]
                chosen_ref[index, side * RANK : (side + 1) * RANK] = picked

    return call(
        body,
        scalars,
        [params, second, grad, totals],
        (),
        [
            jax.ShapeDtypeStruct((3, rows, columns), F32),
            jax.ShapeDtypeStruct((3, 2 * RANK, rows), F32),
        ],
        20 * rows * columns,
        [pltpu.VMEM((columns, rows), F32)],
    )


def local(
    carried,
    norm_gain,
    frozen_key_matrix,
    frozen_value_matrix,
    adapter_params,
    adapter_second,
    right_params,
    right_second,
    row_jobs,
    job_tokens,
    finishing,
    cotangent,
):
    n_data = lax.axis_size("dp")
    core_index = lax.axis_index("tensor")
    core = core_index[None].astype(jnp.int32)
    place = lax.axis_index("dp")
    x_here = carried[0]
    tokens, half = x_here.shape
    width = 2 * half
    block = adapter_params.shape[2]
    kv = frozen_key_matrix.shape[2]
    gain = norm_gain
    key_matrix, value_matrix = frozen_key_matrix[0], frozen_value_matrix[0]
    cot = cotangent[0].reshape(tokens, 2 * kv)
    jobs = row_jobs[0][:, None]

    factors = adapter_params[0, 0].astype(BF16)
    gain_high = gain.astype(BF16)
    gain_low = (gain - gain_high.astype(F32)).astype(BF16)
    gain_rows = width // COLUMNS
    sent = [factors, gain_high.reshape(gain_rows, COLUMNS), gain_low.reshape(gain_rows, COLUMNS)]
    sent = shifted(jnp.concatenate(sent, axis=0), "section", -1)
    factors_next = sent[:block]
    gain_next = sent[block : block + gain_rows].astype(F32) + sent[block + gain_rows :].astype(F32)
    gain_next = gain_next.reshape(1, width)
    part = half // PARTS
    x_parts = [x_here[:, index * part : (index + 1) * part] for index in range(PARTS)]
    x_in = [shifted(value, "section", 1) for value in x_parts]
    up = right_params[0, 0].astype(BF16).reshape(1, -1, 2 * kv)
    rows_local = up.shape[1]
    up = lax.all_to_all(jnp.tile(up, (n_data, 1, 1)), "dp", 0, 0, tiled=True)
    up = up.reshape(FEATURE_WIDTH, 2 * kv)

    both = lax.all_gather(
        jnp.concatenate([factors, after(factors_next, *x_parts)], axis=1), ("dp", "tensor"), axis=0, tiled=True
    )

    leaving = frozen_back(core, cot, key_matrix, value_matrix, half)
    received = [swapped(part) for part in leaving]

    squares = jnp.sum(jnp.square(x_here.astype(F32)), axis=1, keepdims=True)
    rstd = lax.rsqrt((squares + swapped(squares)) / width + 1e-05)

    back_part = back_product(after(core, leaving[0]), cot, up)
    kept, given = normed_by_parity(after(core, back_part), x_here, rstd, gain_next, block)
    taken = swapped(given)
    back = masked(back_part + swapped(back_part), jobs).astype(BF16)
    back_next = shifted(back, "section", -1)

    scaled = frozen_back(
        after(core, back, kept, x_in[0]), cot, key_matrix, value_matrix, half, received, gain
    )
    scaled_next = shifted(scaled, "section", -1)

    down_piece = down_gradient(after(core, scaled), kept, taken, back_next, block)
    down_pieces = lax.all_to_all(down_piece, "dp", 0, 0, tiled=True)

    x_other = [swapped(value) for value in x_in]
    sources = (gain, key_matrix, value_matrix)
    frozen = projected(after(core, down_piece), x_in[0], x_other[0], 0, half, *sources, cot)
    frozen, sums = projected(core, x_in[1], x_other[1], part, half, *sources, cot, frozen)
    low_part = low_rank_down(after(core, frozen), x_in, gain, both)
    low, up_piece, rstd_in, mean = up_gradient(
        core, low_part, swapped(low_part), jobs, cot, back, sums, swapped(sums), width
    )
    up_pieces = up_piece.reshape(n_data, rows_local, 2 * kv)
    up_pieces = lax.all_to_all(up_pieces, "dp", 0, 0, tiled=True)
    mean = shifted(mean, "section", -1)
    kv_out = with_low_rank(after(core, up_piece, scaled_next), frozen, low, up, rstd_in)
    turn = swapped(kv_out[:16, :128])
    down_sum = summed(after(core, turn), down_pieces)
    down_sum = shifted(down_sum, "section", 1)

    input_grad = norm_backward(
        after(core, kv_out), scaled_next, back_next, both, gain_next, x_here, rstd, mean
    )
    kv_out = kv_out.reshape(1, tokens, 2, kv)
    up_sum = jnp.sum(up_pieces.astype(F32), axis=0).reshape(rows_local, 2, kv)

    job_ids = jnp.arange(JOBS, dtype=jnp.int32)
    counts = job_tokens.astype(F32)
    col_job = jnp.arange(COLUMNS, dtype=jnp.int32) % FEATURE_WIDTH // RANK
    column_total = jnp.sum(
        jnp.where(col_job[:, None] == job_ids[None, :], counts[None, :], 0.0), axis=1
    )
    row_job = (place * rows_local + jnp.arange(rows_local, dtype=jnp.int32)) // RANK
    row_count = jnp.sum(
        jnp.where(row_job[:, None] == job_ids[None, :], counts[None, :], 0.0), axis=1
    )
    scalars = jnp.concatenate([after(core, input_grad, up_pieces), finishing.astype(jnp.int32)])
    new_a, chosen = down_optimizer(
        scalars, adapter_params[0], adapter_second[0], down_sum, column_total[None, :]
    )
    new_b = jnp.stack(
        adam_update(
            right_params[0, 0],
            right_params[0, 1],
            right_second[0],
            up_sum / row_count[:, None, None],
        )
    )
    other = swapped(chosen)
    own = core_index == 0
    checkpoint = jnp.concatenate(
        [jnp.where(own, chosen, other), jnp.where(own, other, chosen)], axis=2
    )[None]
    return (kv_out, input_grad[None], new_a[None], new_b[None], checkpoint)


def solution(mesh):
    return jax.shard_map(
        local,
        mesh=mesh,
        in_specs=(
            P("section", "dp", "tensor"),
            P("section", None),
            P("section", None, "tensor"),
            P("section", None, "tensor"),
            P("section", None, ("dp", "tensor"), None),
            P("section", ("dp", "tensor"), None),
            P("section", None, "dp", None, "tensor"),
            P("section", "dp", None, "tensor"),
            P("section", "dp"),
            P(),
            P("section"),
            P("section", "dp", None, "tensor"),
        ),
        out_specs=(
            P("section", "dp", None, "tensor"),
            P("section", "dp", "tensor"),
            P("section", None, ("dp", "tensor"), None),
            P("section", None, "dp", None, "tensor"),
            P("section", None, None, "dp"),
        ),
        check_vma=False,
    )
```

```python
import jax
import jax.numpy as jnp
from jax import lax
from jax.experimental import pallas as pl
from jax.experimental.pallas import tpu as pltpu
from jax.sharding import PartitionSpec as P

JOBS = 8
RANK = 16
ADAM_STEP = 10
ADAPTER_SCALING = 2.0
BETA_ONE = 0.9
BETA_TWO = 0.999
ADAM_EPS = 1e-08
LEARN_RATE = 0.01

FEATURE_WIDTH = JOBS * RANK
COLUMNS = 2 * FEATURE_WIDTH
STEP = 1024
VMEM_LIMIT = 54 * 1024 * 1024
LOW_LIMIT = 54 * 1024 * 1024
FULL_LIMIT = 60 * 1024 * 1024
SMALL_LIMIT = 24 * 1024 * 1024
HINT = 16
TURNS = 0
CHUNKS = 2
PARTS = 2

F32 = jnp.float32
BF16 = jnp.bfloat16


def shifted(value, axis, steps):
    count = lax.axis_size(axis)
    pairs = [(source, (source + steps) % count) for source in range(count)]
    return lax.ppermute(value, axis, pairs)


def swapped(value):
    return shifted(value, "tensor", 1)


def after(value, *others):
    return lax.optimization_barrier((value,) + others)[0]


def adam_update(param, first, second, grad):
    first = BETA_ONE * first + (1.0 - BETA_ONE) * grad
    second = BETA_TWO * second + (1.0 - BETA_TWO) * grad * grad
    first_fix = 1.0 - BETA_ONE**ADAM_STEP
    second_fix = 1.0 - BETA_TWO**ADAM_STEP
    param = param - LEARN_RATE * (first / first_fix) / (jnp.sqrt(second / second_fix) + ADAM_EPS)
    return param, first, second


def rows_dot(left, right):
    return lax.dot_general(left, right, (((0,), (0,)), ((), ())), preferred_element_type=F32)


def columns_dot(left, right):
    return lax.dot_general(left, right, (((1,), (1,)), ((), ())), preferred_element_type=F32)


def dot(left, right):
    return jnp.dot(left, right, preferred_element_type=F32)


def whole(shape):
    return pl.BlockSpec(shape, lambda i, core: (0,) * len(shape))


HBM = pl.BlockSpec(memory_space=pl.ANY)


def call(
    body, core, args, streamed, out_shape, flops, scratch=(), streamed_outs=(), limit=SMALL_LIMIT
):
    outs = jax.tree.leaves(out_shape)
    moved = sum(a.size * a.dtype.itemsize for a in outs + list(args))
    out_specs = [
        HBM if index in streamed_outs else whole(out.shape) for index, out in enumerate(outs)
    ]
    single = not isinstance(out_shape, list)
    return pl.pallas_call(
        body,
        out_shape=out_shape,
        grid_spec=pltpu.PrefetchScalarGridSpec(
            num_scalar_prefetch=1,
            grid=(1,),
            in_specs=[
                HBM if index in streamed else whole(arg.shape) for index, arg in enumerate(args)
            ],
            out_specs=out_specs[0] if single else out_specs,
            scratch_shapes=list(scratch),
        ),
        compiler_params=pltpu.CompilerParams(vmem_limit_bytes=limit),
        cost_estimate=pl.CostEstimate(
            flops=flops // HINT, bytes_accessed=moved // HINT, transcendentals=0
        ),
    )(core, *args)


def started(pairs, sems):
    copies = [
        pltpu.make_async_copy(source, target, sems.at[index])
        for index, (source, target) in enumerate(pairs)
    ]
    for copy in copies:
        copy.start()
    return copies


def lanes_of(index, size=STEP):
    return pl.ds(index * size, size)


def frozen_back(core, cot, key_matrix, value_matrix, half, received=None, gain=None):
    tokens, kv = cot.shape[0], cot.shape[1] // 2
    steps = half // STEP
    own = received is not None
    parts = CHUNKS
    within = steps // parts

    def body(core_ref, cot_ref, key_ref, value_ref, *rest):
        if own:
            received_refs, (gain_ref, *rest) = rest[:parts], rest[parts:]
            out_refs, rest = rest[:1], rest[1:]
        else:
            out_refs, rest = rest[:parts], rest[parts:]
        keys, values, out, key_sems, value_sems, out_sems, *rest = rest
        side = core_ref[0] if own else 1 - core_ref[0]
        base = pl.multiple_of(side * half, half)
        rows = [pl.ds(base + i * STEP, STEP) for i in range(steps)]
        copies = []
        for i in range(steps):
            pairs = [
                (key_ref.at[rows[i]], keys.at[lanes_of(i)], key_sems.at[i]),
                (value_ref.at[rows[i]], values.at[lanes_of(i)], value_sems.at[i]),
            ]
            if own:
                arrived, arrived_sems = rest
                pairs.append(
                    (
                        received_refs[i // within].at[:, lanes_of(i % within)],
                        arrived.at[:, lanes_of(i)],
                        arrived_sems.at[i],
                    )
                )
            copies.append([pltpu.make_async_copy(*pair) for pair in pairs])
            for copy in copies[i]:
                copy.start()
        leaving = []
        for i in range(steps):
            for copy in copies[i]:
                copy.wait()
            total = columns_dot(cot_ref[:, :kv], keys[lanes_of(i)])
            total += columns_dot(cot_ref[:, kv:], values[lanes_of(i)])
            if own:
                total = (total + arrived[:, lanes_of(i)].astype(F32)) * gain_ref[:, rows[i]]
            out[:, lanes_of(i)] = total.astype(BF16)
            if own:
                target = out_refs[0].at[:, lanes_of(i)]
            else:
                target = out_refs[i // within].at[:, lanes_of(i % within)]
            leaving.append(pltpu.make_async_copy(out.at[:, lanes_of(i)], target, out_sems.at[i]))
            leaving[i].start()
        for copy in leaving:
            copy.wait()

    sems = pltpu.SemaphoreType.DMA((steps,))
    args = [cot, key_matrix, value_matrix]
    scratch = [
        pltpu.VMEM((half, kv), BF16),
        pltpu.VMEM((half, kv), BF16),
        pltpu.VMEM((tokens, half), BF16),
        sems,
        sems,
        sems,
    ]
    if own:
        args += [*received, gain]
        scratch += [pltpu.VMEM((tokens, half), BF16), sems]
    piece = jax.ShapeDtypeStruct((tokens, half // parts), BF16)
    return call(
        body,
        core,
        args,
        (1, 2) + tuple(range(3, 3 + parts)) * own,
        jax.ShapeDtypeStruct((tokens, half), BF16) if own else [piece] * parts,
        4 * tokens * half * kv,
        scratch,
        tuple(range(1 if own else parts)),
        VMEM_LIMIT,
    )


def normed_by_parity(core, x, rstd, gain, block):
    tokens, half = x.shape
    steps = half // STEP
    pairs = STEP // (2 * block)
    part = pairs * block

    def body(core_ref, x_ref, rstd_ref, gain_ref, kept_ref, given_ref, xs, kept, given, *sems):
        x_sems, kept_sems, given_sems = sems
        base = pl.multiple_of(core_ref[0] * half, half)
        copies = started(
            [(x_ref.at[:, lanes_of(i)], xs.at[:, lanes_of(i)]) for i in range(steps)], x_sems
        )
        rstd = rstd_ref[...]
        leaving = []
        for i in range(steps):
            copies[i].wait()
            for pair in range(pairs):
                for side in range(2):
                    start = i * STEP + (2 * pair + side) * block
                    normed = xs[:, start : start + block].astype(F32) * rstd
                    normed = (normed * gain_ref[:, pl.ds(base + start, block)]).astype(BF16)
                    out = lanes_of(i * pairs + pair, block)

                    @pl.when(core_ref[0] == side)
                    def _():
                        kept[:, out] = normed

                    @pl.when(core_ref[0] != side)
                    def _():
                        given[:, out] = normed

            for buffer, ref, out_sems in (
                (given, given_ref, given_sems),
                (kept, kept_ref, kept_sems),
            ):
                leaving.append(
                    pltpu.make_async_copy(
                        buffer.at[:, lanes_of(i, part)],
                        ref.at[:, lanes_of(i, part)],
                        out_sems.at[i],
                    )
                )
                leaving[-1].start()
        for copy in leaving:
            copy.wait()

    shape = jax.ShapeDtypeStruct((tokens, half // 2), BF16)
    sems = pltpu.SemaphoreType.DMA((steps,))
    return call(
        body,
        core,
        [x, rstd, gain],
        (0,),
        [shape, shape],
        tokens * half,
        [
            pltpu.VMEM((tokens, half), BF16),
            pltpu.VMEM((tokens, half // 2), BF16),
            pltpu.VMEM((tokens, half // 2), BF16),
            sems,
            sems,
            sems,
        ],
        (0, 1),
    )


def down_gradient(core, kept, taken, back, block):
    tokens, width = kept.shape
    count = width // block
    group = 4
    steps = count // group

    def body(core_ref, kept_ref, taken_ref, back_ref, out_ref, normed, out, in_sems, out_sems):
        copies = started(
            [(kept_ref, normed.at[0]), (taken_ref, normed.at[1])],
            in_sems,
        )
        turned = (ADAPTER_SCALING * back_ref[...].astype(F32)).T.astype(BF16)
        leaving = []
        for side in range(2):
            copies[side].wait()
            owner = core_ref[0] if side == 0 else 1 - core_ref[0]
            for step in range(steps):
                for index in range(step * group, (step + 1) * group):
                    piece = dot(turned, normed[side, :, index * block : (index + 1) * block])
                    out[side * count + index] = piece.astype(BF16)
                copy = pltpu.make_async_copy(
                    out.at[pl.ds(side * count + step * group, group)],
                    out_ref.at[pl.ds(owner * count + step * group, group)],
                    out_sems.at[side * steps + step],
                )
                copy.start()
                leaving.append(copy)
        for copy in leaving:
            copy.wait()

    return call(
        body,
        core,
        [kept, taken, back],
        (0, 1),
        jax.ShapeDtypeStruct((2 * count, COLUMNS, block), BF16),
        4 * tokens * width * COLUMNS,
        [
            pltpu.VMEM((2, tokens, width), BF16),
            pltpu.VMEM((2 * count, COLUMNS, block), BF16),
            pltpu.SemaphoreType.DMA((2,)),
            pltpu.SemaphoreType.DMA((2 * steps,)),
        ],
        (0,),
    )


def projected(core, own, other, start, half, gain, key_matrix, value_matrix, cot, before=None):
    tokens, part = own.shape
    kv = key_matrix.shape[1]
    within = part // STEP
    steps = 2 * within
    last = before is not None

    def body(core_ref, own_ref, other_ref, gain_ref, key_ref, value_ref, *rest):
        if last:
            cot_ref, before_ref, sums_before_ref, *rest = rest
        out_ref, sums_ref, *rest = rest
        held, keys, values, x_sems, key_sems, value_sems = rest
        rows, copies = [], []
        for i in range(steps):
            ref, side = (own_ref, core_ref[0]) if i < within else (other_ref, 1 - core_ref[0])
            first = side * half + start + i % within * STEP
            rows.append(pl.ds(pl.multiple_of(first, STEP), STEP))
            sources = [
                (ref.at[:, lanes_of(i % within)], held.at[:, lanes_of(i)], x_sems),
                (key_ref.at[rows[i]], keys.at[lanes_of(i)], key_sems),
                (value_ref.at[rows[i]], values.at[lanes_of(i)], value_sems),
            ]
            copies.append([pltpu.make_async_copy(a, b, sems.at[i]) for a, b, sems in sources])
            for copy in copies[i]:
                copy.start()
        for i in range(steps):
            for copy in copies[i]:
                copy.wait()
            wide = held[:, lanes_of(i)].astype(F32)
            if i < within:
                square = jnp.sum(wide * wide, axis=1, keepdims=True)
                squares = square if i == 0 else squares + square
            scaled = (wide * gain_ref[:, rows[i]]).astype(BF16)
            for lanes, matrix in ((slice(0, kv), keys), (slice(kv, 2 * kv), values)):
                product = dot(scaled, matrix[lanes_of(i)])
                if i > 0:
                    out_ref[:, lanes] += product
                elif last:
                    out_ref[:, lanes] = before_ref[:, lanes] + product
                else:
                    out_ref[:, lanes] = product
        sums_ref[...] = jnp.broadcast_to(squares, sums_ref.shape)
        if last:
            products = jnp.sum(out_ref[...] * cot_ref[...].astype(F32), axis=1, keepdims=True)
            column = lax.broadcasted_iota(jnp.int32, sums_ref.shape, 1)
            sums_ref[...] = jnp.where(column == 0, squares + sums_before_ref[...], products)

    sems = pltpu.SemaphoreType.DMA((steps,))
    total = jax.ShapeDtypeStruct((tokens, 2 * kv), F32)
    return call(
        body,
        core,
        [own, other, gain, key_matrix, value_matrix] + ([cot, *before] if last else []),
        (0, 1, 3, 4),
        [total, jax.ShapeDtypeStruct((tokens, 2), F32)],
        8 * tokens * part * kv,
        [
            pltpu.VMEM((tokens, 2 * part), BF16),
            pltpu.VMEM((2 * part, kv), BF16),
            pltpu.VMEM((2 * part, kv), BF16),
            sems,
            sems,
            sems,
        ],
        limit=VMEM_LIMIT,
    )


def low_rank_down(core, x, rstd, gain, factors):
    tokens, half = x.shape
    steps = half // STEP

    def body(core_ref, x_ref, rstd_ref, gain_ref, factors_ref, out_ref, held, ours, x_sems, sems):
        base = pl.multiple_of(core_ref[0] * half, half)
        rows = [pl.ds(base + i * STEP, STEP) for i in range(steps)]
        copies = []
        for i in range(steps):
            sources = [
                (x_ref.at[:, lanes_of(i)], held.at[:, lanes_of(i)], x_sems),
                (factors_ref.at[rows[i]], ours.at[lanes_of(i)], sems),
            ]
            copies.append([pltpu.make_async_copy(a, b, c.at[i]) for a, b, c in sources])
            for copy in copies[i]:
                copy.start()
        for i in range(steps):
            for copy in copies[i]:
                copy.wait()
            normed = held[:, lanes_of(i)].astype(F32) * rstd_ref[...] * gain_ref[:, rows[i]]
            product = dot(normed.astype(BF16), ours[lanes_of(i)])
            if i == 0:
                out_ref[...] = product
            else:
                out_ref[...] += product

    sems = pltpu.SemaphoreType.DMA((steps,))
    return call(
        body,
        core,
        [x, rstd, gain, factors],
        (0, 3),
        jax.ShapeDtypeStruct((tokens, COLUMNS), F32),
        2 * tokens * half * COLUMNS,
        [
            pltpu.VMEM((tokens, half), BF16),
            pltpu.VMEM((half, COLUMNS), BF16),
            sems,
            sems,
        ],
        limit=LOW_LIMIT,
    )


def masked(value, jobs):
    column = lax.broadcasted_iota(jnp.int32, value.shape, 1)
    return jnp.where(jobs == (column & (FEATURE_WIDTH - 1)) // RANK, value, 0.0)


def back_product(core, cot, up):
    tokens, kv = cot.shape[0], cot.shape[1] // 2

    def body(core_ref, cot_ref, up_ref, out_ref):
        for side in range(2):
            lanes = lanes_of(side, kv)
            picked = columns_dot(cot_ref[:, lanes], up_ref[:, lanes])
            out_ref[:, side * FEATURE_WIDTH : (side + 1) * FEATURE_WIDTH] = picked

    return call(
        body,
        core,
        [cot, up],
        (),
        jax.ShapeDtypeStruct((tokens, COLUMNS), F32),
        4 * tokens * kv * FEATURE_WIDTH,
    )


def with_low_rank(core, frozen, low, jobs, up, cot, back, sums, other_sums, width):
    tokens, kv = frozen.shape[0], frozen.shape[1] // 2

    def body(core_ref, frozen_ref, low_ref, jobs_ref, up_ref, cot_ref, back_ref, *rest):
        sums_ref, other_sums_ref, out_ref, mean_ref, grad_ref = rest
        sums = sums_ref[...] + other_sums_ref[...]
        rstd = lax.rsqrt(sums[:, :1] / width + 1e-05)
        low = masked(low_ref[...].astype(F32), jobs_ref[...])
        low_products = jnp.sum(low * back_ref[...].astype(F32), axis=1, keepdims=True)
        low = low.astype(BF16)
        mean_ref[...] = (sums[:, 1:2] * rstd + ADAPTER_SCALING * low_products) / width
        for side in range(2):
            lanes = lanes_of(side, kv)
            picked = low[:, side * FEATURE_WIDTH : (side + 1) * FEATURE_WIDTH]
            total = frozen_ref[:, lanes] * rstd
            total += ADAPTER_SCALING * dot(picked, up_ref[:, lanes])
            out_ref[:, lanes] = total.astype(BF16)
            grad = ADAPTER_SCALING * rows_dot(picked, cot_ref[:, lanes])
            grad_ref[:, lanes] = grad.astype(BF16)

    return call(
        body,
        core,
        [frozen, low, jobs, up, cot, back, sums, other_sums],
        (),
        [
            jax.ShapeDtypeStruct(frozen.shape, BF16),
            jax.ShapeDtypeStruct((tokens, 1), F32),
            jax.ShapeDtypeStruct((FEATURE_WIDTH, 2 * kv), BF16),
        ],
        4 * tokens * kv * FEATURE_WIDTH,
        limit=FULL_LIMIT,
    )


def norm_backward(core, scaled, back, factors, gain, x, rstd, mean):
    tokens, half = x.shape
    steps = half // STEP

    def body(core_ref, scaled_ref, back_ref, factors_ref, gain_ref, x_ref, *rest):
        rstd_ref, mean_ref, out_ref, ins, ours, xs, out, in_sems, sems, x_sems, out_sems = rest
        base = pl.multiple_of(core_ref[0] * half, half)
        rows = [pl.ds(base + i * STEP, STEP) for i in range(steps)]
        copies = []
        for i in range(steps):
            lanes = lanes_of(i)
            sources = [
                (factors_ref.at[rows[i]], ours.at[lanes], sems),
                (x_ref.at[:, lanes], xs.at[:, lanes], x_sems),
                (scaled_ref.at[:, lanes], ins.at[:, lanes], in_sems),
            ]
            copies.append([pltpu.make_async_copy(a, b, c.at[i]) for a, b, c in sources])
            for copy in copies[i]:
                copy.start()
        back = back_ref[...]
        rstd = rstd_ref[...]
        shift = rstd * rstd * mean_ref[...]
        leaving = []
        for i in range(steps):
            lanes = lanes_of(i)
            for copy in copies[i]:
                copy.wait()
            low = columns_dot(back, ours[lanes])
            total = ins[:, lanes].astype(F32) + (ADAPTER_SCALING * gain_ref[:, rows[i]]) * low
            out[:, lanes] = (rstd * total - xs[:, lanes].astype(F32) * shift).astype(BF16)
            leaving.append(
                pltpu.make_async_copy(out.at[:, lanes], out_ref.at[:, lanes], out_sems.at[i])
            )
            leaving[i].start()
        for copy in leaving:
            copy.wait()

    sems = pltpu.SemaphoreType.DMA((steps,))
    strip = pltpu.VMEM((tokens, half), BF16)
    return call(
        body,
        core,
        [scaled, back, factors, gain, x, rstd, mean],
        (0, 2, 4),
        jax.ShapeDtypeStruct((tokens, half), BF16),
        2 * tokens * half * COLUMNS,
        [strip, pltpu.VMEM((half, COLUMNS), BF16), strip, strip, sems, sems, sems, sems],
        (0,),
        VMEM_LIMIT,
    )


def summed(core, pieces):
    count, rows, columns = pieces.shape
    steps = 4
    part = rows // steps

    def body(core_ref, pieces_ref, out_ref, held, sems):
        copies = started(
            [
                (pieces_ref.at[:, lanes_of(i, part)], held.at[:, lanes_of(i, part)])
                for i in range(steps)
            ],
            sems,
        )
        for i in range(steps):
            copies[i].wait()
            total = jnp.sum(held[:, lanes_of(i, part)].astype(F32), axis=0)
            out_ref[lanes_of(i, part)] = total.astype(BF16)

    return call(
        body,
        core,
        [pieces],
        (0,),
        jax.ShapeDtypeStruct((rows, columns), BF16),
        pieces.size,
        [pltpu.VMEM(pieces.shape, BF16), pltpu.SemaphoreType.DMA((steps,))],
    )


def down_optimizer(scalars, params, second, grad, totals):
    rows, columns = grad.shape

    def body(scalars_ref, params_ref, second_ref, grad_ref, totals_ref, new_ref, chosen_ref, turned):
        grad = grad_ref[...].astype(F32).T / totals_ref[...]
        new = adam_update(params_ref[0], params_ref[1], second_ref[...], grad)
        job = pl.multiple_of(scalars_ref[1] * RANK, RANK)
        for index, value in enumerate(new):
            new_ref[index] = value
            turned[...] = value.T
            for side in range(2):
                picked = turned[pl.ds(side * FEATURE_WIDTH + job, RANK), :]
                chosen_ref[index, side * RANK : (side + 1) * RANK] = picked

    return call(
        body,
        scalars,
        [params, second, grad, totals],
        (),
        [
            jax.ShapeDtypeStruct((3, rows, columns), F32),
            jax.ShapeDtypeStruct((3, 2 * RANK, rows), F32),
        ],
        20 * rows * columns,
        [pltpu.VMEM((columns, rows), F32)],
    )


def local(
    carried,
    norm_gain,
    frozen_key_matrix,
    frozen_value_matrix,
    adapter_params,
    adapter_second,
    right_params,
    right_second,
    row_jobs,
    job_tokens,
    finishing,
    cotangent,
):
    n_data = lax.axis_size("dp")
    core_index = lax.axis_index("tensor")
    core = core_index[None].astype(jnp.int32)
    place = lax.axis_index("dp")
    x_here = carried[0]
    tokens, half = x_here.shape
    width = 2 * half
    block = adapter_params.shape[2]
    kv = frozen_key_matrix.shape[2]
    gain = norm_gain
    key_matrix, value_matrix = frozen_key_matrix[0], frozen_value_matrix[0]
    cot = cotangent[0].reshape(tokens, 2 * kv)
    jobs = row_jobs[0][:, None]

    factors = adapter_params[0, 0].astype(BF16)
    gain_high = gain.astype(BF16)
    gain_low = (gain - gain_high.astype(F32)).astype(BF16)
    gain_rows = width // COLUMNS
    sent = [factors, gain_high.reshape(gain_rows, COLUMNS), gain_low.reshape(gain_rows, COLUMNS)]
    sent = shifted(jnp.concatenate(sent, axis=0), "section", -1)
    factors_next = sent[:block]
    gain_next = sent[block : block + gain_rows].astype(F32) + sent[block + gain_rows :].astype(F32)
    gain_next = gain_next.reshape(1, width)
    part = half // PARTS
    x_parts = [x_here[:, index * part : (index + 1) * part] for index in range(PARTS)]
    x_in = [shifted(value, "section", 1) for value in x_parts]
    up = right_params[0, 0].astype(BF16).reshape(1, -1, 2 * kv)
    rows_local = up.shape[1]
    up = lax.all_to_all(jnp.tile(up, (n_data, 1, 1)), "dp", 0, 0, tiled=True)
    up = up.reshape(FEATURE_WIDTH, 2 * kv)

    all_next = lax.all_gather(
        after(factors_next, *x_parts), ("dp", "tensor"), axis=0, tiled=True
    )

    leaving = frozen_back(core, cot, key_matrix, value_matrix, half)
    received = [swapped(part) for part in leaving]

    squares = jnp.sum(jnp.square(x_here.astype(F32)), axis=1, keepdims=True)
    rstd = lax.rsqrt((squares + swapped(squares)) / width + 1e-05)

    back_part = back_product(after(core, leaving[0]), cot, up)
    kept, given = normed_by_parity(after(core, back_part), x_here, rstd, gain_next, block)
    taken = swapped(given)
    back = masked(back_part + swapped(back_part), jobs).astype(BF16)
    back_next = shifted(back, "section", -1)

    scaled = frozen_back(
        after(core, back, kept, x_in[0]), cot, key_matrix, value_matrix, half, received, gain
    )
    scaled_next = shifted(scaled, "section", -1)

    down_piece = down_gradient(after(core, scaled), kept, taken, back_next, block)
    down_pieces = lax.all_to_all(down_piece, "dp", 0, 0, tiled=True)

    sources = (gain, key_matrix, value_matrix)
    frozen = projected(
        after(core, down_piece), x_in[0], swapped(x_in[0]), 0, half, *sources, cot
    )
    x_other = swapped(after(x_in[1], frozen[0]))
    low_part = low_rank_down(after(core, frozen), x_here, rstd, gain_next, all_next)
    frozen, sums = projected(after(core, low_part), x_in[1], x_other, part, half, *sources, cot, frozen)

    low = shifted((low_part + swapped(low_part)).astype(BF16), "section", 1)
    kv_out, mean, up_piece = with_low_rank(
        core, frozen, low, jobs, up, cot, back, sums, swapped(sums), width
    )
    mean = shifted(mean, "section", -1)
    up_pieces = up_piece.reshape(n_data, rows_local, 2 * kv)
    up_pieces = lax.all_to_all(up_pieces, "dp", 0, 0, tiled=True)
    down_sum = summed(after(core, up_piece), down_pieces)
    down_sum = shifted(down_sum, "section", 1)

    job_ids = jnp.arange(JOBS, dtype=jnp.int32)
    counts = job_tokens.astype(F32)
    col_job = jnp.arange(COLUMNS, dtype=jnp.int32) % FEATURE_WIDTH // RANK
    column_total = jnp.sum(
        jnp.where(col_job[:, None] == job_ids[None, :], counts[None, :], 0.0), axis=1
    )
    row_job = (place * rows_local + jnp.arange(rows_local, dtype=jnp.int32)) // RANK
    row_count = jnp.sum(
        jnp.where(row_job[:, None] == job_ids[None, :], counts[None, :], 0.0), axis=1
    )
    scalars = jnp.concatenate([after(core, down_sum, up_pieces), finishing.astype(jnp.int32)])
    new_a, chosen = down_optimizer(
        scalars, adapter_params[0], adapter_second[0], down_sum, column_total[None, :]
    )
    input_grad = norm_backward(
        after(core, chosen), scaled_next, back_next, all_next, gain_next, x_here, rstd, mean
    )
    kv_out = kv_out.reshape(1, tokens, 2, kv)
    up_sum = jnp.sum(up_pieces.astype(F32), axis=0).reshape(rows_local, 2, kv)

    new_b = jnp.stack(
        adam_update(
            right_params[0, 0],
            right_params[0, 1],
            right_second[0],
            up_sum / row_count[:, None, None],
        )
    )
    other = swapped(chosen)
    own = core_index == 0
    checkpoint = jnp.concatenate(
        [jnp.where(own, chosen, other), jnp.where(own, other, chosen)], axis=2
    )[None]
    return (kv_out, input_grad[None], new_a[None], new_b[None], checkpoint)


def solution(mesh):
    return jax.shard_map(
        local,
        mesh=mesh,
        in_specs=(
            P("section", "dp", "tensor"),
            P("section", None),
            P("section", None, "tensor"),
            P("section", None, "tensor"),
            P("section", None, ("dp", "tensor"), None),
            P("section", ("dp", "tensor"), None),
            P("section", None, "dp", None, "tensor"),
            P("section", "dp", None, "tensor"),
            P("section", "dp"),
            P(),
            P("section"),
            P("section", "dp", None, "tensor"),
        ),
        out_specs=(
            P("section", "dp", None, "tensor"),
            P("section", "dp", "tensor"),
            P("section", None, ("dp", "tensor"), None),
            P("section", None, "dp", None, "tensor"),
            P("section", None, None, "dp"),
        ),
        check_vma=False,
    )
```

```python
import jax
import jax.numpy as jnp
from jax import lax
from jax.experimental import pallas as pl
from jax.experimental.pallas import tpu as pltpu
from jax.sharding import PartitionSpec as P

JOBS = 8
RANK = 16
ADAM_STEP = 10
ADAPTER_SCALING = 2.0
BETA_ONE = 0.9
BETA_TWO = 0.999
ADAM_EPS = 1e-08
LEARN_RATE = 0.01

FEATURE_WIDTH = JOBS * RANK
COLUMNS = 2 * FEATURE_WIDTH
STEP = 1024
VMEM_LIMIT = 54 * 1024 * 1024
LOW_LIMIT = 54 * 1024 * 1024
FULL_LIMIT = 60 * 1024 * 1024
SMALL_LIMIT = 24 * 1024 * 1024
HINT = 16
TURNS = 0
CHUNKS = 2
PARTS = 2

F32 = jnp.float32
BF16 = jnp.bfloat16


def shifted(value, axis, steps):
    count = lax.axis_size(axis)
    pairs = [(source, (source + steps) % count) for source in range(count)]
    return lax.ppermute(value, axis, pairs)


def swapped(value):
    return shifted(value, "tensor", 1)


def after(value, *others):
    return lax.optimization_barrier((value,) + others)[0]


def adam_update(param, first, second, grad):
    first = BETA_ONE * first + (1.0 - BETA_ONE) * grad
    second = BETA_TWO * second + (1.0 - BETA_TWO) * grad * grad
    first_fix = 1.0 - BETA_ONE**ADAM_STEP
    second_fix = 1.0 - BETA_TWO**ADAM_STEP
    param = param - LEARN_RATE * (first / first_fix) / (jnp.sqrt(second / second_fix) + ADAM_EPS)
    return param, first, second


def rows_dot(left, right):
    return lax.dot_general(left, right, (((0,), (0,)), ((), ())), preferred_element_type=F32)


def columns_dot(left, right):
    return lax.dot_general(left, right, (((1,), (1,)), ((), ())), preferred_element_type=F32)


def dot(left, right):
    return jnp.dot(left, right, preferred_element_type=F32)


def whole(shape):
    return pl.BlockSpec(shape, lambda i, core: (0,) * len(shape))


HBM = pl.BlockSpec(memory_space=pl.ANY)


def call(
    body, core, args, streamed, out_shape, flops, scratch=(), streamed_outs=(), limit=SMALL_LIMIT
):
    outs = jax.tree.leaves(out_shape)
    moved = sum(a.size * a.dtype.itemsize for a in outs + list(args))
    out_specs = [
        HBM if index in streamed_outs else whole(out.shape) for index, out in enumerate(outs)
    ]
    single = not isinstance(out_shape, list)
    return pl.pallas_call(
        body,
        out_shape=out_shape,
        grid_spec=pltpu.PrefetchScalarGridSpec(
            num_scalar_prefetch=1,
            grid=(1,),
            in_specs=[
                HBM if index in streamed else whole(arg.shape) for index, arg in enumerate(args)
            ],
            out_specs=out_specs[0] if single else out_specs,
            scratch_shapes=list(scratch),
        ),
        compiler_params=pltpu.CompilerParams(vmem_limit_bytes=limit),
        cost_estimate=pl.CostEstimate(
            flops=flops // HINT, bytes_accessed=moved // HINT, transcendentals=0
        ),
    )(core, *args)


def started(pairs, sems):
    copies = [
        pltpu.make_async_copy(source, target, sems.at[index])
        for index, (source, target) in enumerate(pairs)
    ]
    for copy in copies:
        copy.start()
    return copies


def lanes_of(index, size=STEP):
    return pl.ds(index * size, size)


def frozen_back(core, cot, key_matrix, value_matrix, half, received=None, gain=None):
    tokens, kv = cot.shape[0], cot.shape[1] // 2
    steps = half // STEP
    own = received is not None
    parts = CHUNKS
    within = steps // parts

    def body(core_ref, cot_ref, key_ref, value_ref, *rest):
        if own:
            received_refs, (gain_ref, *rest) = rest[:parts], rest[parts:]
            out_refs, rest = rest[:1], rest[1:]
        else:
            out_refs, rest = rest[:parts], rest[parts:]
        keys, values, out, key_sems, value_sems, out_sems, *rest = rest
        side = core_ref[0] if own else 1 - core_ref[0]
        base = pl.multiple_of(side * half, half)
        rows = [pl.ds(base + i * STEP, STEP) for i in range(steps)]
        copies = []
        for i in range(steps):
            pairs = [
                (key_ref.at[rows[i]], keys.at[lanes_of(i)], key_sems.at[i]),
                (value_ref.at[rows[i]], values.at[lanes_of(i)], value_sems.at[i]),
            ]
            if own:
                arrived, arrived_sems = rest
                pairs.append(
                    (
                        received_refs[i // within].at[:, lanes_of(i % within)],
                        arrived.at[:, lanes_of(i)],
                        arrived_sems.at[i],
                    )
                )
            copies.append([pltpu.make_async_copy(*pair) for pair in pairs])
            for copy in copies[i]:
                copy.start()
        leaving = []
        for i in range(steps):
            for copy in copies[i]:
                copy.wait()
            total = columns_dot(cot_ref[:, :kv], keys[lanes_of(i)])
            total += columns_dot(cot_ref[:, kv:], values[lanes_of(i)])
            if own:
                total = (total + arrived[:, lanes_of(i)].astype(F32)) * gain_ref[:, rows[i]]
            out[:, lanes_of(i)] = total.astype(BF16)
            if own:
                target = out_refs[0].at[:, lanes_of(i)]
            else:
                target = out_refs[i // within].at[:, lanes_of(i % within)]
            leaving.append(pltpu.make_async_copy(out.at[:, lanes_of(i)], target, out_sems.at[i]))
            leaving[i].start()
        for copy in leaving:
            copy.wait()

    sems = pltpu.SemaphoreType.DMA((steps,))
    args = [cot, key_matrix, value_matrix]
    scratch = [
        pltpu.VMEM((half, kv), BF16),
        pltpu.VMEM((half, kv), BF16),
        pltpu.VMEM((tokens, half), BF16),
        sems,
        sems,
        sems,
    ]
    if own:
        args += [*received, gain]
        scratch += [pltpu.VMEM((tokens, half), BF16), sems]
    piece = jax.ShapeDtypeStruct((tokens, half // parts), BF16)
    return call(
        body,
        core,
        args,
        (1, 2) + tuple(range(3, 3 + parts)) * own,
        jax.ShapeDtypeStruct((tokens, half), BF16) if own else [piece] * parts,
        4 * tokens * half * kv,
        scratch,
        tuple(range(1 if own else parts)),
        VMEM_LIMIT,
    )


def normed_by_parity(core, x, rstd, gain, block):
    tokens, half = x.shape
    steps = half // STEP
    pairs = STEP // (2 * block)
    part = pairs * block

    def body(core_ref, x_ref, rstd_ref, gain_ref, kept_ref, given_ref, xs, kept, given, *sems):
        x_sems, kept_sems, given_sems = sems
        base = pl.multiple_of(core_ref[0] * half, half)
        copies = started(
            [(x_ref.at[:, lanes_of(i)], xs.at[:, lanes_of(i)]) for i in range(steps)], x_sems
        )
        rstd = rstd_ref[...]
        leaving = []
        for i in range(steps):
            copies[i].wait()
            for pair in range(pairs):
                for side in range(2):
                    start = i * STEP + (2 * pair + side) * block
                    normed = xs[:, start : start + block].astype(F32) * rstd
                    normed = (normed * gain_ref[:, pl.ds(base + start, block)]).astype(BF16)
                    out = lanes_of(i * pairs + pair, block)

                    @pl.when(core_ref[0] == side)
                    def _():
                        kept[:, out] = normed

                    @pl.when(core_ref[0] != side)
                    def _():
                        given[:, out] = normed

            for buffer, ref, out_sems in (
                (given, given_ref, given_sems),
                (kept, kept_ref, kept_sems),
            ):
                leaving.append(
                    pltpu.make_async_copy(
                        buffer.at[:, lanes_of(i, part)],
                        ref.at[:, lanes_of(i, part)],
                        out_sems.at[i],
                    )
                )
                leaving[-1].start()
        for copy in leaving:
            copy.wait()

    shape = jax.ShapeDtypeStruct((tokens, half // 2), BF16)
    sems = pltpu.SemaphoreType.DMA((steps,))
    return call(
        body,
        core,
        [x, rstd, gain],
        (0,),
        [shape, shape],
        tokens * half,
        [
            pltpu.VMEM((tokens, half), BF16),
            pltpu.VMEM((tokens, half // 2), BF16),
            pltpu.VMEM((tokens, half // 2), BF16),
            sems,
            sems,
            sems,
        ],
        (0, 1),
    )


def down_gradient(core, kept, taken, back, block):
    tokens, width = kept.shape
    count = width // block
    group = 4
    steps = count // group

    def body(core_ref, kept_ref, taken_ref, back_ref, out_ref, normed, out, in_sems, out_sems):
        copies = started(
            [(kept_ref, normed.at[0]), (taken_ref, normed.at[1])],
            in_sems,
        )
        turned = (ADAPTER_SCALING * back_ref[...].astype(F32)).T.astype(BF16)
        leaving = []
        for side in range(2):
            copies[side].wait()
            owner = core_ref[0] if side == 0 else 1 - core_ref[0]
            for step in range(steps):
                for index in range(step * group, (step + 1) * group):
                    piece = dot(turned, normed[side, :, index * block : (index + 1) * block])
                    out[side * count + index] = piece.astype(BF16)
                copy = pltpu.make_async_copy(
                    out.at[pl.ds(side * count + step * group, group)],
                    out_ref.at[pl.ds(owner * count + step * group, group)],
                    out_sems.at[side * steps + step],
                )
                copy.start()
                leaving.append(copy)
        for copy in leaving:
            copy.wait()

    return call(
        body,
        core,
        [kept, taken, back],
        (0, 1),
        jax.ShapeDtypeStruct((2 * count, COLUMNS, block), BF16),
        4 * tokens * width * COLUMNS,
        [
            pltpu.VMEM((2, tokens, width), BF16),
            pltpu.VMEM((2 * count, COLUMNS, block), BF16),
            pltpu.SemaphoreType.DMA((2,)),
            pltpu.SemaphoreType.DMA((2 * steps,)),
        ],
        (0,),
    )


def projected(core, own, other, start, half, gain, key_matrix, value_matrix, cot, before=None):
    tokens, part = own.shape
    kv = key_matrix.shape[1]
    within = part // STEP
    steps = 2 * within
    last = before is not None

    def body(core_ref, own_ref, other_ref, gain_ref, key_ref, value_ref, *rest):
        if last:
            cot_ref, before_ref, sums_before_ref, *rest = rest
        out_ref, sums_ref, *rest = rest
        held, keys, values, x_sems, key_sems, value_sems = rest
        rows, copies = [], []
        for i in range(steps):
            ref, side = (own_ref, core_ref[0]) if i < within else (other_ref, 1 - core_ref[0])
            first = side * half + start + i % within * STEP
            rows.append(pl.ds(pl.multiple_of(first, STEP), STEP))
            sources = [
                (ref.at[:, lanes_of(i % within)], held.at[:, lanes_of(i)], x_sems),
                (key_ref.at[rows[i]], keys.at[lanes_of(i)], key_sems),
                (value_ref.at[rows[i]], values.at[lanes_of(i)], value_sems),
            ]
            copies.append([pltpu.make_async_copy(a, b, sems.at[i]) for a, b, sems in sources])
            for copy in copies[i]:
                copy.start()
        for i in range(steps):
            for copy in copies[i]:
                copy.wait()
            wide = held[:, lanes_of(i)].astype(F32)
            if i < within:
                square = jnp.sum(wide * wide, axis=1, keepdims=True)
                squares = square if i == 0 else squares + square
            scaled = (wide * gain_ref[:, rows[i]]).astype(BF16)
            for lanes, matrix in ((slice(0, kv), keys), (slice(kv, 2 * kv), values)):
                product = dot(scaled, matrix[lanes_of(i)])
                if i > 0:
                    out_ref[:, lanes] += product
                elif last:
                    out_ref[:, lanes] = before_ref[:, lanes] + product
                else:
                    out_ref[:, lanes] = product
        sums_ref[...] = jnp.broadcast_to(squares, sums_ref.shape)
        if last:
            products = jnp.sum(out_ref[...] * cot_ref[...].astype(F32), axis=1, keepdims=True)
            column = lax.broadcasted_iota(jnp.int32, sums_ref.shape, 1)
            sums_ref[...] = jnp.where(column == 0, squares + sums_before_ref[...], products)

    sems = pltpu.SemaphoreType.DMA((steps,))
    total = jax.ShapeDtypeStruct((tokens, 2 * kv), F32)
    return call(
        body,
        core,
        [own, other, gain, key_matrix, value_matrix] + ([cot, *before] if last else []),
        (0, 1, 3, 4),
        [total, jax.ShapeDtypeStruct((tokens, 2), F32)],
        8 * tokens * part * kv,
        [
            pltpu.VMEM((tokens, 2 * part), BF16),
            pltpu.VMEM((2 * part, kv), BF16),
            pltpu.VMEM((2 * part, kv), BF16),
            sems,
            sems,
            sems,
        ],
        limit=VMEM_LIMIT,
    )


def low_rank_down(core, x, rstd, gain, factors):
    tokens, half = x.shape
    steps = half // STEP

    def body(core_ref, x_ref, rstd_ref, gain_ref, factors_ref, out_ref, held, ours, x_sems, sems):
        base = pl.multiple_of(core_ref[0] * half, half)
        rows = [pl.ds(base + i * STEP, STEP) for i in range(steps)]
        copies = []
        for i in range(steps):
            sources = [
                (x_ref.at[:, lanes_of(i)], held.at[:, lanes_of(i)], x_sems),
                (factors_ref.at[rows[i]], ours.at[lanes_of(i)], sems),
            ]
            copies.append([pltpu.make_async_copy(a, b, c.at[i]) for a, b, c in sources])
            for copy in copies[i]:
                copy.start()
        for i in range(steps):
            for copy in copies[i]:
                copy.wait()
            normed = held[:, lanes_of(i)].astype(F32) * rstd_ref[...] * gain_ref[:, rows[i]]
            product = dot(normed.astype(BF16), ours[lanes_of(i)])
            if i == 0:
                out_ref[...] = product
            else:
                out_ref[...] += product

    sems = pltpu.SemaphoreType.DMA((steps,))
    return call(
        body,
        core,
        [x, rstd, gain, factors],
        (0, 3),
        jax.ShapeDtypeStruct((tokens, COLUMNS), F32),
        2 * tokens * half * COLUMNS,
        [
            pltpu.VMEM((tokens, half), BF16),
            pltpu.VMEM((half, COLUMNS), BF16),
            sems,
            sems,
        ],
        limit=LOW_LIMIT,
    )


def masked(value, jobs):
    column = lax.broadcasted_iota(jnp.int32, value.shape, 1)
    return jnp.where(jobs == (column & (FEATURE_WIDTH - 1)) // RANK, value, 0.0)


def back_product(core, cot, up):
    tokens, kv = cot.shape[0], cot.shape[1] // 2

    def body(core_ref, cot_ref, up_ref, out_ref):
        for side in range(2):
            lanes = lanes_of(side, kv)
            picked = columns_dot(cot_ref[:, lanes], up_ref[:, lanes])
            out_ref[:, side * FEATURE_WIDTH : (side + 1) * FEATURE_WIDTH] = picked

    return call(
        body,
        core,
        [cot, up],
        (),
        jax.ShapeDtypeStruct((tokens, COLUMNS), F32),
        4 * tokens * kv * FEATURE_WIDTH,
    )


def with_low_rank(core, frozen, low, jobs, up, cot, back, sums, other_sums, width):
    tokens, kv = frozen.shape[0], frozen.shape[1] // 2

    def body(core_ref, frozen_ref, low_ref, jobs_ref, up_ref, cot_ref, back_ref, *rest):
        sums_ref, other_sums_ref, out_ref, mean_ref, grad_ref = rest
        sums = sums_ref[...] + other_sums_ref[...]
        rstd = lax.rsqrt(sums[:, :1] / width + 1e-05)
        low = masked(low_ref[...].astype(F32), jobs_ref[...])
        low_products = jnp.sum(low * back_ref[...].astype(F32), axis=1, keepdims=True)
        low = low.astype(BF16)
        mean_ref[...] = (sums[:, 1:2] * rstd + ADAPTER_SCALING * low_products) / width
        for side in range(2):
            lanes = lanes_of(side, kv)
            picked = low[:, side * FEATURE_WIDTH : (side + 1) * FEATURE_WIDTH]
            total = frozen_ref[:, lanes] * rstd
            total += ADAPTER_SCALING * dot(picked, up_ref[:, lanes])
            out_ref[:, lanes] = total.astype(BF16)
            grad = ADAPTER_SCALING * rows_dot(picked, cot_ref[:, lanes])
            grad_ref[:, lanes] = grad.astype(BF16)

    return call(
        body,
        core,
        [frozen, low, jobs, up, cot, back, sums, other_sums],
        (),
        [
            jax.ShapeDtypeStruct(frozen.shape, BF16),
            jax.ShapeDtypeStruct((tokens, 1), F32),
            jax.ShapeDtypeStruct((FEATURE_WIDTH, 2 * kv), BF16),
        ],
        4 * tokens * kv * FEATURE_WIDTH,
        limit=FULL_LIMIT,
    )


def norm_backward(core, scaled, back, factors, gain, x, rstd, mean):
    tokens, half = x.shape
    steps = half // STEP

    def body(core_ref, scaled_ref, back_ref, factors_ref, gain_ref, x_ref, *rest):
        rstd_ref, mean_ref, out_ref, ins, ours, xs, out, in_sems, sems, x_sems, out_sems = rest
        base = pl.multiple_of(core_ref[0] * half, half)
        rows = [pl.ds(base + i * STEP, STEP) for i in range(steps)]
        copies = []
        for i in range(steps):
            lanes = lanes_of(i)
            sources = [
                (factors_ref.at[rows[i]], ours.at[lanes], sems),
                (x_ref.at[:, lanes], xs.at[:, lanes], x_sems),
                (scaled_ref.at[:, lanes], ins.at[:, lanes], in_sems),
            ]
            copies.append([pltpu.make_async_copy(a, b, c.at[i]) for a, b, c in sources])
            for copy in copies[i]:
                copy.start()
        back = back_ref[...]
        rstd = rstd_ref[...]
        shift = rstd * rstd * mean_ref[...]
        leaving = []
        for i in range(steps):
            lanes = lanes_of(i)
            for copy in copies[i]:
                copy.wait()
            low = columns_dot(back, ours[lanes])
            total = ins[:, lanes].astype(F32) + (ADAPTER_SCALING * gain_ref[:, rows[i]]) * low
            out[:, lanes] = (rstd * total - xs[:, lanes].astype(F32) * shift).astype(BF16)
            leaving.append(
                pltpu.make_async_copy(out.at[:, lanes], out_ref.at[:, lanes], out_sems.at[i])
            )
            leaving[i].start()
        for copy in leaving:
            copy.wait()

    sems = pltpu.SemaphoreType.DMA((steps,))
    strip = pltpu.VMEM((tokens, half), BF16)
    return call(
        body,
        core,
        [scaled, back, factors, gain, x, rstd, mean],
        (0, 2, 4),
        jax.ShapeDtypeStruct((tokens, half), BF16),
        2 * tokens * half * COLUMNS,
        [strip, pltpu.VMEM((half, COLUMNS), BF16), strip, strip, sems, sems, sems, sems],
        (0,),
        VMEM_LIMIT,
    )


def summed(core, pieces):
    count, rows, columns = pieces.shape
    steps = 4
    part = rows // steps

    def body(core_ref, pieces_ref, out_ref, held, sems):
        copies = started(
            [
                (pieces_ref.at[:, lanes_of(i, part)], held.at[:, lanes_of(i, part)])
                for i in range(steps)
            ],
            sems,
        )
        for i in range(steps):
            copies[i].wait()
            total = jnp.sum(held[:, lanes_of(i, part)].astype(F32), axis=0)
            out_ref[lanes_of(i, part)] = total.astype(BF16)

    return call(
        body,
        core,
        [pieces],
        (0,),
        jax.ShapeDtypeStruct((rows, columns), BF16),
        pieces.size,
        [pltpu.VMEM(pieces.shape, BF16), pltpu.SemaphoreType.DMA((steps,))],
    )


def down_optimizer(scalars, params, second, grad, totals):
    rows, columns = grad.shape

    def body(scalars_ref, params_ref, second_ref, grad_ref, totals_ref, new_ref, chosen_ref, turned):
        grad = grad_ref[...].astype(F32).T / totals_ref[...]
        new = adam_update(params_ref[0], params_ref[1], second_ref[...], grad)
        job = pl.multiple_of(scalars_ref[1] * RANK, RANK)
        for index, value in enumerate(new):
            new_ref[index] = value
            turned[...] = value.T
            for side in range(2):
                picked = turned[pl.ds(side * FEATURE_WIDTH + job, RANK), :]
                chosen_ref[index, side * RANK : (side + 1) * RANK] = picked

    return call(
        body,
        scalars,
        [params, second, grad, totals],
        (),
        [
            jax.ShapeDtypeStruct((3, rows, columns), F32),
            jax.ShapeDtypeStruct((3, 2 * RANK, rows), F32),
        ],
        20 * rows * columns,
        [pltpu.VMEM((columns, rows), F32)],
    )


def local(
    carried,
    norm_gain,
    frozen_key_matrix,
    frozen_value_matrix,
    adapter_params,
    adapter_second,
    right_params,
    right_second,
    row_jobs,
    job_tokens,
    finishing,
    cotangent,
):
    n_data = lax.axis_size("dp")
    core_index = lax.axis_index("tensor")
    core = core_index[None].astype(jnp.int32)
    place = lax.axis_index("dp")
    x_here = carried[0]
    tokens, half = x_here.shape
    width = 2 * half
    block = adapter_params.shape[2]
    kv = frozen_key_matrix.shape[2]
    gain = norm_gain
    key_matrix, value_matrix = frozen_key_matrix[0], frozen_value_matrix[0]
    cot = cotangent[0].reshape(tokens, 2 * kv)
    jobs = row_jobs[0][:, None]

    factors = adapter_params[0, 0].astype(BF16)
    gain_high = gain.astype(BF16)
    gain_low = (gain - gain_high.astype(F32)).astype(BF16)
    gain_rows = width // COLUMNS
    sent = [factors, gain_high.reshape(gain_rows, COLUMNS), gain_low.reshape(gain_rows, COLUMNS)]
    sent = shifted(jnp.concatenate(sent, axis=0), "section", -1)
    factors_next = sent[:block]
    gain_next = sent[block : block + gain_rows].astype(F32) + sent[block + gain_rows :].astype(F32)
    gain_next = gain_next.reshape(1, width)
    part = half // PARTS
    x_parts = [x_here[:, index * part : (index + 1) * part] for index in range(PARTS)]
    x_in = [shifted(value, "section", 1) for value in x_parts]
    up = right_params[0, 0].astype(BF16).reshape(1, -1, 2 * kv)
    rows_local = up.shape[1]
    up = lax.all_to_all(jnp.tile(up, (n_data, 1, 1)), "dp", 0, 0, tiled=True)
    up = up.reshape(FEATURE_WIDTH, 2 * kv)

    all_next = lax.all_gather(
        after(factors_next, *x_parts), ("dp", "tensor"), axis=0, tiled=True
    )

    leaving = frozen_back(core, cot, key_matrix, value_matrix, half)
    received = [swapped(part) for part in leaving]

    squares = jnp.sum(jnp.square(x_here.astype(F32)), axis=1, keepdims=True)
    rstd = lax.rsqrt((squares + swapped(squares)) / width + 1e-05)

    back_part = back_product(after(core, leaving[0]), cot, up)
    kept, given = normed_by_parity(after(core, back_part), x_here, rstd, gain_next, block)
    taken = swapped(given)
    back = masked(back_part + swapped(back_part), jobs).astype(BF16)
    back_next = shifted(back, "section", -1)

    scaled = frozen_back(
        after(core, back, kept, x_in[0], jobs), cot, key_matrix, value_matrix, half, received, gain
    )
    scaled_next = shifted(scaled, "section", -1)

    down_piece = down_gradient(after(core, scaled), kept, taken, back_next, block)
    down_pieces = lax.all_to_all(down_piece, "dp", 0, 0, tiled=True)

    sources = (gain, key_matrix, value_matrix)
    frozen = projected(
        after(core, down_piece), x_in[0], swapped(x_in[0]), 0, half, *sources, cot
    )
    x_other = swapped(after(x_in[1], frozen[0]))
    low_part = low_rank_down(after(core, frozen), x_here, rstd, gain_next, all_next)
    frozen, sums = projected(after(core, low_part), x_in[1], x_other, part, half, *sources, cot, frozen)

    low = shifted((low_part + swapped(low_part)).astype(BF16), "section", 1)
    kv_out, mean, up_piece = with_low_rank(
        core, frozen, low, jobs, up, cot, back, sums, swapped(sums), width
    )
    mean = shifted(mean, "section", -1)
    up_pieces = up_piece.reshape(n_data, rows_local, 2 * kv)
    up_pieces = lax.all_to_all(up_pieces, "dp", 0, 0, tiled=True)
    down_sum = summed(after(core, up_piece), down_pieces)
    down_sum = shifted(down_sum, "section", 1)

    job_ids = jnp.arange(JOBS, dtype=jnp.int32)
    counts = job_tokens.astype(F32)
    col_job = jnp.arange(COLUMNS, dtype=jnp.int32) % FEATURE_WIDTH // RANK
    column_total = jnp.sum(
        jnp.where(col_job[:, None] == job_ids[None, :], counts[None, :], 0.0), axis=1
    )
    row_job = (place * rows_local + jnp.arange(rows_local, dtype=jnp.int32)) // RANK
    row_count = jnp.sum(
        jnp.where(row_job[:, None] == job_ids[None, :], counts[None, :], 0.0), axis=1
    )
    scalars = jnp.concatenate([after(core, down_sum, up_pieces), finishing.astype(jnp.int32)])
    new_a, chosen = down_optimizer(
        scalars, adapter_params[0], adapter_second[0], down_sum, column_total[None, :]
    )
    kv_out = kv_out.reshape(1, tokens, 2, kv)
    up_sum = jnp.sum(up_pieces.astype(F32), axis=0).reshape(rows_local, 2, kv)

    new_b = jnp.stack(
        adam_update(
            right_params[0, 0],
            right_params[0, 1],
            right_second[0],
            up_sum / row_count[:, None, None],
        )
    )

    input_grad = norm_backward(
        after(core, chosen, new_b),
        scaled_next,
        back_next,
        all_next,
        gain_next,
        x_here,
        rstd,
        mean,
    )

    other = swapped(chosen)
    own = core_index == 0
    checkpoint = jnp.concatenate(
        [jnp.where(own, chosen, other), jnp.where(own, other, chosen)], axis=2
    )[None]
    return (kv_out, input_grad[None], new_a[None], new_b[None], checkpoint)


def solution(mesh):
    return jax.shard_map(
        local,
        mesh=mesh,
        in_specs=(
            P("section", "dp", "tensor"),
            P("section", None),
            P("section", None, "tensor"),
            P("section", None, "tensor"),
            P("section", None, ("dp", "tensor"), None),
            P("section", ("dp", "tensor"), None),
            P("section", None, "dp", None, "tensor"),
            P("section", "dp", None, "tensor"),
            P("section", "dp"),
            P(),
            P("section"),
            P("section", "dp", None, "tensor"),
        ),
        out_specs=(
            P("section", "dp", None, "tensor"),
            P("section", "dp", "tensor"),
            P("section", None, ("dp", "tensor"), None),
            P("section", None, "dp", None, "tensor"),
            P("section", None, None, "dp"),
        ),
        check_vma=False,
    )
```
